512 devices in a mesh: dp: 8 (over y, core), ctx: 64 (over z, x).
Axes of the slice: x: 4, y: 4, z: 16, core: 2. Of those that a mesh axis runs over, the one named last changes fastest.
Arguments:
- features_in: bfloat16 [1536, 65536], P(None, ('dp', 'ctx')), parts along dimension 1, may hold values from -6 to 6
- short_weight: float32 [1536, 3], replicated, may hold values from -3.5 to 3.5
- long_filter: float32 [512, 8192], P(None, 'ctx'), may hold values from -3.5 to 3.5
- skip_gain: float32 [512], replicated, may hold values from -1 to 1
Outputs:
- mixed_out: float32 [512, 65536], P(None, ('dp', 'ctx')), parts along dimension 1
The draws below stay inside these ranges and needn't reach their ends.
There are 8 independent parts, one for each index of `dp`. The reference program is written for one: setup_inputs(seed, part) draws one part's arguments, and reference() takes and returns one part's arrays. A program takes and returns all parts, laid end to end along the dimension named above; an argument that names none is the same for every part. Nothing has to cross between parts.
All inputs are finite; a program needn't handle non-finite values.
Results may differ from the reference program's by a relative error of at most 0.0003.
Values may be sent and summed in bfloat16 or wider, within the bound.
A program may use at most 64 MiB of HBM per device.

```python
import math
import jax
import jax.numpy as jnp

CHANNELS = 512
SHORT = 3
TOKENS = 8192


def draw_long_filter(key, part):
    key = jax.random.fold_in(key, 7)
    key_taps, key_pick, key_slow, key_fast = jax.random.split(key, 4)
    share = 0.5
    taps = jnp.clip(jax.random.normal(key_taps, (CHANNELS, TOKENS), jnp.float32), -3.5, 3.5)
    choose_fast = jax.random.uniform(key_pick, (CHANNELS, 1), jnp.float32) < share
    slow_rate = jnp.exp(jax.random.uniform(key_slow, (CHANNELS, 1), jnp.float32, math.log(0.1 / TOKENS), math.log(1.0 / TOKENS)))
    fast_rate = jnp.exp(jax.random.uniform(key_fast, (CHANNELS, 1), jnp.float32, math.log(1.0 / 40.0), math.log(1.0 / 10.0)))
    rates = jnp.where(choose_fast, fast_rate, slow_rate)
    scaling = jnp.sqrt(jnp.expm1(-2.0 * rates) / jnp.expm1(-2.0 * rates * TOKENS))
    positions = jnp.arange(TOKENS, dtype=jnp.float32)[None, :]
    return taps * scaling * jnp.exp(-rates * positions)


def block_scale(rng, extent, cuts, smallest, high):
    factor_of = 1.0
    for axis_at, parts in cuts:
        heights = jax.random.uniform(jax.random.fold_in(jax.random.fold_in(rng, 6), axis_at), (parts,), jnp.float32, smallest / len(cuts), high / len(cuts))
        factor_of = factor_of * jnp.repeat(jnp.exp(heights), extent[axis_at] // parts).reshape((-1,) + (1,) * (len(extent) - 1 - axis_at))
    return factor_of


def scatter_about(key, dims, deviation, reach, shards=(), kind=jnp.bfloat16):
    entries = jax.random.normal(key, dims, jnp.float32) * deviation
    if len(shards) > 0:
        entries = block_scale(key, dims, shards, -0.22, 0.18) * entries
    return jnp.clip(entries, min=-reach, max=reach).astype(kind)


def setup_inputs(seed: int = 0, part: int = 0) -> dict:
    key_of = jax.random.split(jax.random.key(seed), 5)
    part_keys = jax.random.split(jax.random.fold_in(key_of[4], part), 5)
    features_in = scatter_about(part_keys[0], (3 * CHANNELS, TOKENS), 1.0, 6.0, ((1, 64),))
    short_weight = scatter_about(key_of[1], (3 * CHANNELS, SHORT), SHORT ** -0.5, 3.5, (), jnp.float32)
    long_filter = draw_long_filter(jax.random.fold_in(key_of[4], 71), part)
    skip_gain = jnp.clip(jax.random.uniform(key_of[3], (CHANNELS,), jnp.float32, -1.0, 1.0), -1.0, 1.0)
    return dict(features_in=features_in, short_weight=short_weight, long_filter=long_filter, skip_gain=skip_gain)


def reference(features_in, short_weight, long_filter, skip_gain):
    length = features_in.shape[1]
    channel_count = long_filter.shape[0]
    tap_count = short_weight.shape[1]
    widened = jnp.pad(features_in.astype(jnp.float32), ((0, 0), (tap_count - 1, 0)))
    featurized = jnp.zeros((3 * channel_count, length), jnp.float32)
    for offset in range(tap_count):
        start = tap_count - 1 - offset
        featurized = featurized + short_weight[:, offset][:, None] * widened[:, start:start + length]
    query_part = featurized[:channel_count]
    key_part = featurized[channel_count:2 * channel_count]
    value_part = featurized[2 * channel_count:]
    gated_input = key_part * value_part
    padded_size = 2 * length
    spectrum = jnp.fft.rfft(gated_input, n=padded_size) * jnp.fft.rfft(long_filter, n=padded_size)
    convolved = jnp.fft.irfft(spectrum, n=padded_size)[:, :length]
    convolved = convolved + skip_gain[:, None] * gated_input
    return query_part * convolved
```

```python
import functools
import math

import jax
import jax.numpy as jnp
import numpy as np
from jax import lax
from jax.experimental import pallas as pl
from jax.experimental.pallas import tpu as pltpu
from jax.sharding import PartitionSpec as P

MESH = pl.DeviceIdType.MESH
F32, BF16 = jnp.float32, jnp.bfloat16
RINGS = (16, 4)
CTX = RINGS[0] * RINGS[1]
LANES = 128
OWN = 8
LIFT = 2.0**7.5
SLOT = 16


def coded(value, largest):
    ratio = jnp.where(largest > 1e-30, LIFT / jnp.maximum(largest, 1e-30), 0.0)
    power = value * ratio
    for _ in range(4):
        power = power * power
    return jnp.where(value < 0, -power, power)


def decoded(code):
    size = jnp.abs(code)
    root = jnp.exp(jnp.log(jnp.maximum(size, 1e-37)) * (1.0 / 16.0)) * (1.0 / LIFT)
    root = jnp.where(size > 1e-37, root, 0.0)
    return jnp.where(code < 0, -root, root)


def farthest_first(index, extent):
    half, step = extent // 2, (index + 1) // 2
    return half + step * (1 - 2 * (index % 2))


def each_peer(visit):
    me = lax.axis_index("ctx")
    at_z, at_x = me // RINGS[1], me % RINGS[1]

    def one(index, carry):
        to_z = (at_z + farthest_first(index // RINGS[1], RINGS[0])) % RINGS[0]
        to_x = (at_x + farthest_first(index % RINGS[1], RINGS[1])) % RINGS[1]
        visit(to_z * RINGS[1] + to_x)
        return carry

    lax.fori_loop(0, CTX - 1, one, 0)


def send_blocks(*exchanges):
    me = lax.axis_index("ctx")

    def visit(peer):
        for source, target, sent, landed in exchanges:
            pltpu.make_async_remote_copy(
                src_ref=source.at[peer],
                dst_ref=target.at[me],
                send_sem=sent,
                recv_sem=landed,
                device_id={"ctx": peer},
                device_id_type=MESH,
            ).start()

    each_peer(visit)
    for source, target, _, landed in exchanges:
        pltpu.make_async_copy(source.at[me], target.at[me], landed).start()


def wait_landed(target, landed):
    pltpu.make_async_copy(target, target, landed).wait()


def wait_sent(source, sent):
    part = source.at[pl.ds(0, CTX - 1)]
    pltpu.make_async_copy(part, part, sent).wait()


def split(value):
    high = value.astype(BF16)
    return high, (value - high.astype(F32)).astype(BF16)


def spectrum(blocks, across, inner, turn_re, turn_im):
    high, low = split(jnp.concatenate(blocks, axis=1))
    outer = jnp.dot(across, jnp.concatenate([high, low, high, low], axis=0), preferred_element_type=F32)
    rows = []
    for c in range(OWN):
        part = outer[:, c * LANES : (c + 1) * LANES]
        re, im = part[:CTX], part[CTX:]
        rows.append(jnp.concatenate([re * turn_re - im * turn_im, re * turn_im + im * turn_re], axis=1))
    high, low = split(jnp.concatenate(rows, axis=0))
    return jnp.dot(jnp.concatenate([high, low, high], axis=1), inner, preferred_element_type=F32)


def inverse(product, across, inner, turn_re, turn_im):
    high, low = split(product)
    mixed = jnp.dot(jnp.concatenate([high, low, high], axis=1), inner, preferred_element_type=F32)
    columns = []
    for c in range(OWN):
        part = mixed[c * CTX : (c + 1) * CTX]
        re, im = part[:, :LANES], part[:, LANES:]
        columns.append(jnp.concatenate([re * turn_re + im * turn_im, im * turn_re - re * turn_im], axis=0))
    high, low = split(jnp.concatenate(columns, axis=1))
    return jnp.dot(across, jnp.concatenate([high, low, high], axis=0), preferred_element_type=F32)


def lane_of(shape):
    return lax.broadcasted_iota(jnp.int32, shape, len(shape) - 1)


def kernel(
    feat_hbm, short_hbm, filt_hbm, skip_hbm, fwd_across_hbm, fwd_inner_hbm, inv_inner_hbm, inv_across_hbm, turn_hbm,
    out_ref,
    feat, short, filt, skip, fwd_across, fwd_inner, inv_inner, inv_across, turn,
    edge_rows, edge_wide, plane, plane_h,
    gate_src, edge_src, filt_src, gate_dst, edge_dst, filt_dst,
    conv_src, peak_src, conv_dst, peak_dst, query_tail,
    load_sem, sent, landed,
):
    me = lax.axis_index("ctx")
    barrier = pltpu.get_barrier_semaphore()
    each_peer(lambda peer: pl.semaphore_signal(barrier, inc=1, device_id={"ctx": peer}, device_id_type=MESH))

    pairs = (
        (feat_hbm, feat), (short_hbm, short), (filt_hbm, filt), (skip_hbm, skip), (fwd_across_hbm, fwd_across),
        (fwd_inner_hbm, fwd_inner), (inv_inner_hbm, inv_inner), (inv_across_hbm, inv_across), (turn_hbm, turn),
    )
    loads = [pltpu.make_async_copy(source, target, load_sem.at[i]) for i, (source, target) in enumerate(pairs)]
    for load in loads:
        load.start()
    for load in loads:
        load.wait()

    count = OWN * CTX
    chunk = 8 * OWN
    lane = lane_of((chunk, LANES))

    def local_feature(row):
        rows = pl.ds(row, chunk)
        value = feat[rows, :].astype(F32)
        taps = short[rows, :]
        once, twice = pltpu.roll(value, 1, axis=1), pltpu.roll(value, 2, axis=1)
        near = taps[:, 1:2] * once
        far = taps[:, 2:3] * twice
        zero = jnp.zeros_like(value)
        inside = taps[:, 0:1] * value + jnp.where(lane >= 1, near, zero) + jnp.where(lane >= 2, far, zero)
        beyond = jnp.where(lane < 1, near, zero) + jnp.where(lane < 2, far, zero)
        return inside, beyond

    for i in range(count // chunk):
        row = i * chunk
        zero = jnp.zeros((chunk, LANES), F32)
        key, key_beyond = local_feature(count + row)
        value, value_beyond = local_feature(2 * count + row)
        gated = key * value
        gated = jnp.where(lane >= 2, gated, zero)
        taps = filt[pl.ds(row, chunk), :]
        gated_peak = jnp.max(jnp.abs(gated), axis=1, keepdims=True)
        taps_peak = jnp.max(jnp.abs(taps), axis=1, keepdims=True)
        edge = (
            jnp.where(lane < 2, key, zero)
            + pltpu.roll(jnp.where(lane < 2, value, zero), 2, axis=1)
            + pltpu.roll(key_beyond, 4, axis=1)
            + pltpu.roll(value_beyond, 6, axis=1)
        )
        edge = jnp.where(lane == 8, gated_peak, jnp.where(lane == 9, taps_peak, edge))
        edge_rows[pl.ds(row, chunk), :] = edge
        owners = pl.ds(i * 8, 8)
        gate_src[owners] = coded(gated, gated_peak).reshape(8, OWN, LANES).astype(BF16)
        filt_src[owners] = coded(taps, taps_peak).reshape(8, OWN, LANES).astype(BF16)

    wide = edge_rows[pl.ds(0, CTX, stride=OWN), :]
    for c in range(1, OWN):
        wide = wide + pltpu.roll(edge_rows[pl.ds(c, CTX, stride=OWN), :], SLOT * c, axis=1)
    edge_wide[...] = wide
    for q in range(CTX):
        edge_src[q] = edge_wide[q : q + 1, :]

    pl.semaphore_wait(barrier, CTX - 1)
    send_blocks((gate_src, gate_dst, sent.at[0], landed.at[0]), (edge_src, edge_dst, sent.at[1], landed.at[1]))
    send_blocks((filt_src, filt_dst, sent.at[2], landed.at[2]))
    tail_copy = pltpu.make_async_remote_copy(
        src_ref=feat.at[pl.ds(0, count)],
        dst_ref=query_tail,
        send_sem=sent.at[5],
        recv_sem=landed.at[5],
        device_id={"ctx": (me + 1) % CTX},
        device_id_type=MESH,
    )
    tail_copy.start()

    turn_re, turn_im = turn[:CTX], turn[CTX:]
    wait_landed(gate_dst, landed.at[0])
    wait_landed(edge_dst, landed.at[1])
    for p in range(CTX):
        edge_wide[p : p + 1, :] = edge_dst[p]
    for i in range(8):
        part = decoded(gate_dst[pl.ds(i * 8, 8)].astype(F32))
        plane[pl.ds(i * chunk, chunk), :] = part.reshape(chunk, LANES)
    edge = edge_wide[...]
    row_of = lax.broadcasted_iota(jnp.int32, (CTX, LANES), 0)
    before = jnp.where(row_of >= 1, pltpu.roll(edge, 1, axis=0), 0.0)
    whole = edge + pltpu.roll(before, LANES - 4, axis=1)
    first = whole * pltpu.roll(whole, LANES - 2, axis=1)
    lane = lane_of((CTX, LANES))
    blocks = []
    for c in range(OWN):
        at = SLOT * c
        block = plane[pl.ds(c, CTX, stride=OWN), :] * edge[:, at + 8 : at + 9]
        block = jnp.where(lane == 0, first[:, at : at + 1], block)
        blocks.append(jnp.where(lane == 1, first[:, at + 1 : at + 2], block))
    seen = spectrum(blocks, fwd_across[...], fwd_inner[...], turn_re, turn_im)

    wait_landed(filt_dst, landed.at[2])
    for i in range(8):
        part = decoded(filt_dst[pl.ds(i * 8, 8)].astype(F32))
        plane_h[pl.ds(i * chunk, chunk), :] = part.reshape(chunk, LANES)
    taps = [plane_h[pl.ds(c, CTX, stride=OWN), :] * edge[:, SLOT * c + 9 : SLOT * c + 10] for c in range(OWN)]
    response = spectrum(taps, fwd_across[...], fwd_inner[...], turn_re, turn_im)
    s_re, s_im = seen[:, :LANES], seen[:, LANES:]
    r_re, r_im = response[:, :LANES], response[:, LANES:]
    product = jnp.concatenate([s_re * r_re - s_im * r_im, s_re * r_im + s_im * r_re], axis=1)
    result = inverse(product, inv_across[...], inv_inner[...], turn_re, turn_im)

    peaks = jnp.zeros((CTX, LANES), F32)
    for c in range(OWN):
        part = result[:, c * LANES : (c + 1) * LANES] + skip[me * OWN + c] * blocks[c]
        peak = jnp.max(jnp.abs(part), axis=1, keepdims=True)
        peaks = jnp.where(lane == c, peak, peaks)
        plane[pl.ds(c, CTX, stride=OWN), :] = coded(part, peak)
    edge_wide[...] = peaks
    for q in range(CTX):
        peak_src[q] = edge_wide[q : q + 1, :]
    for i in range(8):
        conv_src[pl.ds(i * 8, 8)] = plane[pl.ds(i * chunk, chunk), :].reshape(8, OWN, LANES).astype(BF16)

    send_blocks((conv_src, conv_dst, sent.at[3], landed.at[3]), (peak_src, peak_dst, sent.at[4], landed.at[4]))

    tail_copy.wait_recv()
    lane = lane_of((chunk, LANES))
    keep = jnp.where(me > 0, 1.0, 0.0)
    for i in range(count // chunk):
        rows = pl.ds(i * chunk, chunk)
        value, tail = feat[rows, :].astype(F32), query_tail[rows, :].astype(F32) * keep
        taps = short[rows, :]
        query = taps[:, 0:1] * value
        for step in (1, 2):
            moved = jnp.where(lane < step, pltpu.roll(tail, step, axis=1), pltpu.roll(value, step, axis=1))
            query = query + taps[:, step : step + 1] * moved
        plane_h[rows, :] = query

    wait_landed(conv_dst, landed.at[3])
    wait_landed(peak_dst, landed.at[4])
    shape = (8, OWN, LANES)
    mine = lane_of(shape) == lax.broadcasted_iota(jnp.int32, shape, 1)
    for i in range(8):
        rows = pl.ds(i * chunk, chunk)
        peak = jnp.broadcast_to(peak_dst[pl.ds(i * 8, 8)], shape)
        peak = jnp.sum(jnp.where(mine, peak, 0.0), axis=2, keepdims=True)
        part = decoded(conv_dst[pl.ds(i * 8, 8)].astype(F32)) * peak
        out_ref[rows, :] = plane_h[rows, :] * part.reshape(chunk, LANES)

    for slot, source in enumerate((gate_src, edge_src, filt_src, conv_src, peak_src)):
        wait_sent(source, sent.at[slot])
    tail_copy.wait_send()


def halves(table):
    high = table.astype(jnp.bfloat16)
    return high, (table - high.astype(np.float64)).astype(jnp.bfloat16)


def tables():
    points = 2 * CTX * LANES
    j, s, k1, k2 = np.arange(CTX), np.arange(LANES), np.arange(CTX) + 0.5, np.arange(LANES)
    outer = 2 * math.pi / LANES * np.outer(k1, j)
    high, low = halves(np.concatenate([np.cos(outer), -np.sin(outer)], axis=0))
    fwd_across = np.concatenate([high, high, low, low], axis=1)
    high, low = halves(np.concatenate([np.cos(outer.T), -np.sin(outer.T)], axis=1) * (2.0 / points))
    inv_across = np.concatenate([high, high, low], axis=1)
    inner = 2 * math.pi / LANES * (np.outer(s, k2) % LANES)
    cos, sin = np.cos(inner), np.sin(inner)
    high, low = halves(np.block([[cos, -sin], [sin, cos]]))
    fwd_inner = np.concatenate([high, high, low], axis=0)
    high, low = halves(np.block([[cos, sin], [-sin, cos]]))
    inv_inner = np.concatenate([high, high, low], axis=0)
    angle = 2 * math.pi / points * np.outer(k1, s)
    turn = np.concatenate([np.cos(angle), -np.sin(angle)], axis=0).astype(np.float32)
    return fwd_across, fwd_inner, inv_inner, inv_across, turn


def solution(mesh):
    constants = tables()

    def body(features_in, short_weight, long_filter, skip_gain):
        operands = (features_in, short_weight, long_filter, skip_gain, *map(jnp.asarray, constants))
        count = long_filter.shape[0]
        rows = (CTX, OWN, LANES)
        row = (CTX, 1, LANES)
        own_copies = [
            (pltpu.SMEM if value.ndim == 1 else pltpu.VMEM)(value.shape, value.dtype) for value in operands
        ]
        scratch = own_copies + [
            pltpu.VMEM((count, LANES), F32),
            pltpu.VMEM((CTX, LANES), F32),
            pltpu.VMEM((count, LANES), F32),
            pltpu.VMEM((count, LANES), F32),
            pltpu.VMEM(rows, BF16), pltpu.VMEM(row, F32), pltpu.VMEM(rows, BF16),
            pltpu.VMEM(rows, BF16), pltpu.VMEM(row, F32), pltpu.VMEM(rows, BF16),
            pltpu.VMEM(rows, BF16), pltpu.VMEM(row, F32),
            pltpu.VMEM(rows, BF16), pltpu.VMEM(row, F32),
            pltpu.VMEM((count, LANES), BF16),
            pltpu.SemaphoreType.DMA((len(operands),)),
            pltpu.SemaphoreType.DMA((6,)),
            pltpu.SemaphoreType.DMA((6,)),
        ]
        return pl.pallas_call(
            kernel,
            out_shape=jax.ShapeDtypeStruct((count, LANES), F32),
            in_specs=[pl.BlockSpec(memory_space=pl.ANY)] * len(operands),
            out_specs=pl.BlockSpec(memory_space=pltpu.VMEM),
            scratch_shapes=scratch,
            compiler_params=pltpu.CompilerParams(
                collective_id=0, has_side_effects=True, vmem_limit_bytes=48 * 1024 * 1024
            ),
        )(*operands)

    return jax.shard_map(
        body,
        mesh=mesh,
        in_specs=(P(None, ("dp", "ctx")), P(), P(None, "ctx"), P()),
        out_specs=P(None, ("dp", "ctx")),
        check_vma=False,
    )
```

```python
import functools
import math

import jax
import jax.numpy as jnp
import numpy as np
from jax import lax
from jax.experimental import pallas as pl
from jax.experimental.pallas import tpu as pltpu
from jax.sharding import PartitionSpec as P

MESH = pl.DeviceIdType.MESH
F32, BF16 = jnp.float32, jnp.bfloat16
RINGS = (16, 4)
CTX = RINGS[0] * RINGS[1]
LANES = 128
OWN = 8
LIFT = 2.0**7.5
SLOT = 16


def coded(value, largest):
    ratio = jnp.where(largest > 1e-30, LIFT / jnp.maximum(largest, 1e-30), 0.0)
    power = value * ratio
    for _ in range(4):
        power = power * power
    return jnp.where(value < 0, -power, power)


def decoded(code):
    size = jnp.abs(code)
    root = jnp.exp(jnp.log(jnp.maximum(size, 1e-37)) * (1.0 / 16.0)) * (1.0 / LIFT)
    root = jnp.where(size > 1e-37, root, 0.0)
    return jnp.where(code < 0, -root, root)


def farthest_first(index, extent):
    half, step = extent // 2, (index + 1) // 2
    return half + step * (1 - 2 * (index % 2))


def each_peer(visit):
    me = lax.axis_index("ctx")
    at_z, at_x = me // RINGS[1], me % RINGS[1]

    def one(index, carry):
        to_z = (at_z + farthest_first(index // RINGS[1], RINGS[0])) % RINGS[0]
        to_x = (at_x + farthest_first(index % RINGS[1], RINGS[1])) % RINGS[1]
        visit(to_z * RINGS[1] + to_x)
        return carry

    lax.fori_loop(0, CTX - 1, one, 0)


def send_blocks(*exchanges):
    me = lax.axis_index("ctx")

    def visit(peer):
        for source, target, sent, landed in exchanges:
            pltpu.make_async_remote_copy(
                src_ref=source.at[peer],
                dst_ref=target.at[me],
                send_sem=sent,
                recv_sem=landed,
                device_id={"ctx": peer},
                device_id_type=MESH,
            ).start()

    each_peer(visit)
    for source, target, _, landed in exchanges:
        pltpu.make_async_copy(source.at[me], target.at[me], landed).start()


def wait_landed(target, landed):
    pltpu.make_async_copy(target, target, landed).wait()


def wait_sent(source, sent):
    part = source.at[pl.ds(0, CTX - 1)]
    pltpu.make_async_copy(part, part, sent).wait()


def split(value):
    high = value.astype(BF16)
    return high, (value - high.astype(F32)).astype(BF16)


def spectrum(blocks, across, inner, turn_re, turn_im):
    high, low = split(jnp.concatenate(blocks, axis=1))
    outer = jnp.dot(across, jnp.concatenate([high, low, high, low], axis=0), preferred_element_type=F32)
    rows = []
    for c in range(OWN):
        part = outer[:, c * LANES : (c + 1) * LANES]
        re, im = part[:CTX], part[CTX:]
        rows.append(jnp.concatenate([re * turn_re - im * turn_im, re * turn_im + im * turn_re], axis=1))
    high, low = split(jnp.concatenate(rows, axis=0))
    return jnp.dot(jnp.concatenate([high, low, high], axis=1), inner, preferred_element_type=F32)


def inverse(product, across, inner, turn_re, turn_im):
    high, low = split(product)
    mixed = jnp.dot(jnp.concatenate([high, low, high], axis=1), inner, preferred_element_type=F32)
    columns = []
    for c in range(OWN):
        part = mixed[c * CTX : (c + 1) * CTX]
        re, im = part[:, :LANES], part[:, LANES:]
        columns.append(jnp.concatenate([re * turn_re + im * turn_im, im * turn_re - re * turn_im], axis=0))
    high, low = split(jnp.concatenate(columns, axis=1))
    return jnp.dot(across, jnp.concatenate([high, low, high], axis=0), preferred_element_type=F32)


def lane_of(shape):
    return lax.broadcasted_iota(jnp.int32, shape, len(shape) - 1)


def kernel(
    feat_hbm, short_hbm, filt_hbm, skip_hbm, fwd_across_hbm, fwd_inner_hbm, inv_inner_hbm, inv_across_hbm, turn_hbm,
    out_ref,
    feat, short_flat, filt, skip, fwd_across, fwd_inner, inv_inner, inv_across, turn,
    short, edge_rows, edge_wide, plane, plane_h,
    gate_src, edge_src, filt_src, gate_dst, edge_dst, filt_dst,
    conv_src, peak_src, conv_dst, peak_dst, query_tail,
    load_sem, sent, landed,
):
    me = lax.axis_index("ctx")
    barrier = pltpu.get_barrier_semaphore()
    each_peer(lambda peer: pl.semaphore_signal(barrier, inc=1, device_id={"ctx": peer}, device_id_type=MESH))

    pairs = (
        (feat_hbm, feat), (short_hbm, short_flat), (filt_hbm, filt), (skip_hbm, skip), (fwd_across_hbm, fwd_across),
        (fwd_inner_hbm, fwd_inner), (inv_inner_hbm, inv_inner), (inv_across_hbm, inv_across), (turn_hbm, turn),
    )
    loads = [pltpu.make_async_copy(source, target, load_sem.at[i]) for i, (source, target) in enumerate(pairs)]
    for load in loads:
        load.start()
    for load in loads:
        load.wait()

    count = OWN * CTX
    chunk = 8 * OWN
    lane = lane_of((chunk, LANES))
    for i in range(3 * count // LANES):
        taps = jnp.concatenate([short_flat[:, i * LANES : (i + 1) * LANES], jnp.zeros((5, LANES), F32)], axis=0)
        short[pl.ds(i * LANES, LANES), :] = taps.T

    def local_feature(row):
        rows = pl.ds(row, chunk)
        value = feat[rows, :].astype(F32)
        taps = short[rows, :]
        once, twice = pltpu.roll(value, 1, axis=1), pltpu.roll(value, 2, axis=1)
        near = taps[:, 1:2] * once
        far = taps[:, 2:3] * twice
        zero = jnp.zeros_like(value)
        inside = taps[:, 0:1] * value + jnp.where(lane >= 1, near, zero) + jnp.where(lane >= 2, far, zero)
        beyond = jnp.where(lane < 1, near, zero) + jnp.where(lane < 2, far, zero)
        return inside, beyond

    for i in range(count // chunk):
        row = i * chunk
        zero = jnp.zeros((chunk, LANES), F32)
        key, key_beyond = local_feature(count + row)
        value, value_beyond = local_feature(2 * count + row)
        gated = key * value
        gated = jnp.where(lane >= 2, gated, zero)
        taps = filt[pl.ds(row, chunk), :]
        gated_peak = jnp.max(jnp.abs(gated), axis=1, keepdims=True)
        taps_peak = jnp.max(jnp.abs(taps), axis=1, keepdims=True)
        edge = (
            jnp.where(lane < 2, key, zero)
            + pltpu.roll(jnp.where(lane < 2, value, zero), 2, axis=1)
            + pltpu.roll(key_beyond, 4, axis=1)
            + pltpu.roll(value_beyond, 6, axis=1)
        )
        edge = jnp.where(lane == 8, gated_peak, jnp.where(lane == 9, taps_peak, edge))
        edge_rows[pl.ds(row, chunk), :] = edge
        owners = pl.ds(i * 8, 8)
        gate_src[owners] = coded(gated, gated_peak).reshape(8, OWN, LANES).astype(BF16)
        filt_src[owners] = coded(taps, taps_peak).reshape(8, OWN, LANES).astype(BF16)

    wide = edge_rows[pl.ds(0, CTX, stride=OWN), :]
    for c in range(1, OWN):
        wide = wide + pltpu.roll(edge_rows[pl.ds(c, CTX, stride=OWN), :], SLOT * c, axis=1)
    edge_wide[...] = wide
    for q in range(CTX):
        edge_src[q] = edge_wide[q : q + 1, :]

    pl.semaphore_wait(barrier, CTX - 1)
    send_blocks((gate_src, gate_dst, sent.at[0], landed.at[0]), (edge_src, edge_dst, sent.at[1], landed.at[1]))
    send_blocks((filt_src, filt_dst, sent.at[2], landed.at[2]))
    tail_copy = pltpu.make_async_remote_copy(
        src_ref=feat.at[pl.ds(0, count)],
        dst_ref=query_tail,
        send_sem=sent.at[5],
        recv_sem=landed.at[5],
        device_id={"ctx": (me + 1) % CTX},
        device_id_type=MESH,
    )
    tail_copy.start()

    turn_re, turn_im = turn[:CTX], turn[CTX:]
    wait_landed(gate_dst, landed.at[0])
    wait_landed(edge_dst, landed.at[1])
    for p in range(CTX):
        edge_wide[p : p + 1, :] = edge_dst[p]
    for i in range(8):
        part = decoded(gate_dst[pl.ds(i * 8, 8)].astype(F32))
        plane[pl.ds(i * chunk, chunk), :] = part.reshape(chunk, LANES)
    edge = edge_wide[...]
    row_of = lax.broadcasted_iota(jnp.int32, (CTX, LANES), 0)
    before = jnp.where(row_of >= 1, pltpu.roll(edge, 1, axis=0), 0.0)
    whole = edge + pltpu.roll(before, LANES - 4, axis=1)
    first = whole * pltpu.roll(whole, LANES - 2, axis=1)
    lane = lane_of((CTX, LANES))
    blocks = []
    for c in range(OWN):
        at = SLOT * c
        block = plane[pl.ds(c, CTX, stride=OWN), :] * edge[:, at + 8 : at + 9]
        block = jnp.where(lane == 0, first[:, at : at + 1], block)
        blocks.append(jnp.where(lane == 1, first[:, at + 1 : at + 2], block))
    seen = spectrum(blocks, fwd_across[...], fwd_inner[...], turn_re, turn_im)

    wait_landed(filt_dst, landed.at[2])
    for i in range(8):
        part = decoded(filt_dst[pl.ds(i * 8, 8)].astype(F32))
        plane_h[pl.ds(i * chunk, chunk), :] = part.reshape(chunk, LANES)
    taps = [plane_h[pl.ds(c, CTX, stride=OWN), :] * edge[:, SLOT * c + 9 : SLOT * c + 10] for c in range(OWN)]
    response = spectrum(taps, fwd_across[...], fwd_inner[...], turn_re, turn_im)
    s_re, s_im = seen[:, :LANES], seen[:, LANES:]
    r_re, r_im = response[:, :LANES], response[:, LANES:]
    product = jnp.concatenate([s_re * r_re - s_im * r_im, s_re * r_im + s_im * r_re], axis=1)
    result = inverse(product, inv_across[...], inv_inner[...], turn_re, turn_im)

    peaks = jnp.zeros((CTX, LANES), F32)
    for c in range(OWN):
        part = result[:, c * LANES : (c + 1) * LANES] + skip[me * OWN + c] * blocks[c]
        peak = jnp.max(jnp.abs(part), axis=1, keepdims=True)
        peaks = jnp.where(lane == c, peak, peaks)
        plane[pl.ds(c, CTX, stride=OWN), :] = coded(part, peak)
    edge_wide[...] = peaks
    for q in range(CTX):
        peak_src[q] = edge_wide[q : q + 1, :]
    for i in range(8):
        conv_src[pl.ds(i * 8, 8)] = plane[pl.ds(i * chunk, chunk), :].reshape(8, OWN, LANES).astype(BF16)

    send_blocks((conv_src, conv_dst, sent.at[3], landed.at[3]), (peak_src, peak_dst, sent.at[4], landed.at[4]))

    tail_copy.wait_recv()
    lane = lane_of((chunk, LANES))
    keep = jnp.where(me > 0, 1.0, 0.0)
    for i in range(count // chunk):
        rows = pl.ds(i * chunk, chunk)
        value, tail = feat[rows, :].astype(F32), query_tail[rows, :].astype(F32) * keep
        taps = short[rows, :]
        query = taps[:, 0:1] * value
        for step in (1, 2):
            moved = jnp.where(lane < step, pltpu.roll(tail, step, axis=1), pltpu.roll(value, step, axis=1))
            query = query + taps[:, step : step + 1] * moved
        plane_h[rows, :] = query

    wait_landed(conv_dst, landed.at[3])
    wait_landed(peak_dst, landed.at[4])
    shape = (8, OWN, LANES)
    mine = lane_of(shape) == lax.broadcasted_iota(jnp.int32, shape, 1)
    for i in range(8):
        rows = pl.ds(i * chunk, chunk)
        peak = jnp.broadcast_to(peak_dst[pl.ds(i * 8, 8)], shape)
        peak = jnp.sum(jnp.where(mine, peak, 0.0), axis=2, keepdims=True)
        part = decoded(conv_dst[pl.ds(i * 8, 8)].astype(F32)) * peak
        out_ref[rows, :] = plane_h[rows, :] * part.reshape(chunk, LANES)

    for slot, source in enumerate((gate_src, edge_src, filt_src, conv_src, peak_src)):
        wait_sent(source, sent.at[slot])
    tail_copy.wait_send()


def halves(table):
    high = table.astype(jnp.bfloat16)
    return high, (table - high.astype(np.float64)).astype(jnp.bfloat16)


def tables():
    points = 2 * CTX * LANES
    j, s, k1, k2 = np.arange(CTX), np.arange(LANES), np.arange(CTX) + 0.5, np.arange(LANES)
    outer = 2 * math.pi / LANES * np.outer(k1, j)
    high, low = halves(np.concatenate([np.cos(outer), -np.sin(outer)], axis=0))
    fwd_across = np.concatenate([high, high, low, low], axis=1)
    high, low = halves(np.concatenate([np.cos(outer.T), -np.sin(outer.T)], axis=1) * (2.0 / points))
    inv_across = np.concatenate([high, high, low], axis=1)
    inner = 2 * math.pi / LANES * (np.outer(s, k2) % LANES)
    cos, sin = np.cos(inner), np.sin(inner)
    high, low = halves(np.block([[cos, -sin], [sin, cos]]))
    fwd_inner = np.concatenate([high, high, low], axis=0)
    high, low = halves(np.block([[cos, sin], [-sin, cos]]))
    inv_inner = np.concatenate([high, high, low], axis=0)
    angle = 2 * math.pi / points * np.outer(k1, s)
    turn = np.concatenate([np.cos(angle), -np.sin(angle)], axis=0).astype(np.float32)
    return fwd_across, fwd_inner, inv_inner, inv_across, turn


def solution(mesh):
    constants = tables()

    def body(features_in, short_weight, long_filter, skip_gain):
        operands = (features_in, short_weight.T, long_filter, skip_gain, *map(jnp.asarray, constants))
        count = long_filter.shape[0]
        rows = (CTX, OWN, LANES)
        row = (CTX, 1, LANES)
        own_copies = [
            (pltpu.SMEM if value.ndim == 1 else pltpu.VMEM)(value.shape, value.dtype) for value in operands
        ]
        scratch = own_copies + [
            pltpu.VMEM((3 * count, 8), F32),
            pltpu.VMEM((count, LANES), F32),
            pltpu.VMEM((CTX, LANES), F32),
            pltpu.VMEM((count, LANES), F32),
            pltpu.VMEM((count, LANES), F32),
            pltpu.VMEM(rows, BF16), pltpu.VMEM(row, F32), pltpu.VMEM(rows, BF16),
            pltpu.VMEM(rows, BF16), pltpu.VMEM(row, F32), pltpu.VMEM(rows, BF16),
            pltpu.VMEM(rows, BF16), pltpu.VMEM(row, F32),
            pltpu.VMEM(rows, BF16), pltpu.VMEM(row, F32),
            pltpu.VMEM((count, LANES), BF16),
            pltpu.SemaphoreType.DMA((len(operands),)),
            pltpu.SemaphoreType.DMA((6,)),
            pltpu.SemaphoreType.DMA((6,)),
        ]
        return pl.pallas_call(
            kernel,
            out_shape=jax.ShapeDtypeStruct((count, LANES), F32),
            in_specs=[pl.BlockSpec(memory_space=pltpu.HBM)] * len(operands),
            out_specs=pl.BlockSpec(memory_space=pltpu.VMEM),
            scratch_shapes=scratch,
            compiler_params=pltpu.CompilerParams(
                collective_id=0, has_side_effects=True, vmem_limit_bytes=60 * 1024 * 1024
            ),
        )(*operands)

    return jax.shard_map(
        body,
        mesh=mesh,
        in_specs=(P(None, ("dp", "ctx")), P(), P(None, "ctx"), P()),
        out_specs=P(None, ("dp", "ctx")),
        check_vma=False,
    )
```

```python
import functools
import math

import jax
import jax.numpy as jnp
import numpy as np
from jax import lax
from jax.experimental import pallas as pl
from jax.experimental.pallas import tpu as pltpu
from jax.sharding import PartitionSpec as P

MESH = pl.DeviceIdType.MESH
F32, BF16 = jnp.float32, jnp.bfloat16
RINGS = (16, 4)
CTX = RINGS[0] * RINGS[1]
SHARE = 8
LANES = 128
OWN = 8
LIFT = 2.0**7.5
SLOT = 16


def coded(value, largest):
    ratio = jnp.where(largest > 1e-30, LIFT / jnp.maximum(largest, 1e-30), 0.0)
    power = value * ratio
    for _ in range(4):
        power = power * power
    return jnp.where(value < 0, -power, power)


def decoded(code):
    size = jnp.abs(code)
    root = jnp.exp(jnp.log(jnp.maximum(size, 1e-37)) * (1.0 / 16.0)) * (1.0 / LIFT)
    root = jnp.where(size > 1e-37, root, 0.0)
    return jnp.where(code < 0, -root, root)


def farthest_first(index, extent):
    half, step = extent // 2, (index + 1) // 2
    return half + step * (1 - 2 * (index % 2))


def each_peer(visit):
    me = lax.axis_index("ctx")
    at_z, at_x = me // RINGS[1], me % RINGS[1]

    def one(index, carry):
        to_z = (at_z + farthest_first(index // RINGS[1], RINGS[0])) % RINGS[0]
        to_x = (at_x + farthest_first(index % RINGS[1], RINGS[1])) % RINGS[1]
        visit(to_z * RINGS[1] + to_x)
        return carry

    lax.fori_loop(0, CTX - 1, one, 0)


def remote(source, target, sent, landed, **where):
    return pltpu.make_async_remote_copy(
        src_ref=source, dst_ref=target, send_sem=sent, recv_sem=landed, device_id=where, device_id_type=MESH
    )


def wait_bytes(ref, semaphore):
    pltpu.make_async_copy(ref, ref, semaphore).wait()


def split(value):
    high = value.astype(BF16)
    return high, (value - high.astype(F32)).astype(BF16)


def spectrum(blocks, across, inner, turn_re, turn_im):
    high, low = split(jnp.concatenate(blocks, axis=1))
    outer = jnp.dot(across, jnp.concatenate([high, low, high, low], axis=0), preferred_element_type=F32)
    rows = []
    for c in range(OWN):
        part = outer[:, c * LANES : (c + 1) * LANES]
        re, im = part[:CTX], part[CTX:]
        rows.append(jnp.concatenate([re * turn_re - im * turn_im, re * turn_im + im * turn_re], axis=1))
    high, low = split(jnp.concatenate(rows, axis=0))
    return jnp.dot(jnp.concatenate([high, low, high], axis=1), inner, preferred_element_type=F32)


def inverse(product, across, inner, turn_re, turn_im):
    high, low = split(product)
    mixed = jnp.dot(jnp.concatenate([high, low, high], axis=1), inner, preferred_element_type=F32)
    columns = []
    for c in range(OWN):
        part = mixed[c * CTX : (c + 1) * CTX]
        re, im = part[:, :LANES], part[:, LANES:]
        columns.append(jnp.concatenate([re * turn_re + im * turn_im, im * turn_re - re * turn_im], axis=0))
    high, low = split(jnp.concatenate(columns, axis=1))
    return jnp.dot(across, jnp.concatenate([high, low, high], axis=0), preferred_element_type=F32)


def lane_of(shape):
    return lax.broadcasted_iota(jnp.int32, shape, len(shape) - 1)


GATE, EDGE, FILT, CONV, PEAK, TAIL, SIDE, SLOTS = 0, 1, 2, 3, 4, 5, 6, 6 + SHARE


def kernel(
    feat_hbm, short_hbm, filt_hbm, skip_hbm, fwd_across_hbm, fwd_inner_hbm, inv_inner_hbm, inv_across_hbm, turn_hbm,
    out_ref,
    feat, short_flat, filt, skip, fwd_across, fwd_inner, inv_inner, inv_across, turn,
    short, edge_rows, edge_wide, plane, plane_h, query_part,
    gate_src, edge_src, filt_src, gate_dst, edge_dst, filt_dst,
    conv_src, peak_src, conv_dst, peak_dst, query_tail,
    load_sem, sent, landed, direct,
):
    me, part_at = lax.axis_index("ctx"), lax.axis_index("dp")
    group = (part_at - me) % SHARE
    barrier = pltpu.get_barrier_semaphore()
    each_peer(lambda peer: pl.semaphore_signal(barrier, inc=1, device_id={"ctx": peer}, device_id_type=MESH))
    for step in range(1, SHARE):
        pl.semaphore_signal(barrier, inc=1, device_id={"dp": (part_at + step) % SHARE}, device_id_type=MESH)

    pairs = (
        (feat_hbm, feat), (short_hbm, short_flat), (filt_hbm, filt), (skip_hbm, skip), (fwd_across_hbm, fwd_across),
        (fwd_inner_hbm, fwd_inner), (inv_inner_hbm, inv_inner), (inv_across_hbm, inv_across), (turn_hbm, turn),
    )
    loads = [pltpu.make_async_copy(source, target, load_sem.at[i]) for i, (source, target) in enumerate(pairs)]
    for load in loads:
        load.start()
    for load in loads:
        load.wait()

    count = OWN * CTX
    chunk = 8 * OWN
    lane = lane_of((chunk, LANES))
    for i in range(3 * count // LANES):
        taps = jnp.concatenate([short_flat[:, i * LANES : (i + 1) * LANES], jnp.zeros((5, LANES), F32)], axis=0)
        short[pl.ds(i * LANES, LANES), :] = taps.T

    def local_feature(row):
        rows = pl.ds(row, chunk)
        value = feat[rows, :].astype(F32)
        taps = short[rows, :]
        once, twice = pltpu.roll(value, 1, axis=1), pltpu.roll(value, 2, axis=1)
        near = taps[:, 1:2] * once
        far = taps[:, 2:3] * twice
        zero = jnp.zeros_like(value)
        inside = taps[:, 0:1] * value + jnp.where(lane >= 1, near, zero) + jnp.where(lane >= 2, far, zero)
        beyond = jnp.where(lane < 1, near, zero) + jnp.where(lane < 2, far, zero)
        return inside, beyond

    for i in range(count // chunk):
        row = i * chunk
        zero = jnp.zeros((chunk, LANES), F32)
        query, query_beyond = local_feature(row)
        query_part[pl.ds(row, chunk), :] = query
        key, key_beyond = local_feature(count + row)
        value, value_beyond = local_feature(2 * count + row)
        gated = key * value
        gated = jnp.where(lane >= 2, gated, zero)
        taps = filt[pl.ds(row, chunk), :]
        gated_peak = jnp.max(jnp.abs(gated), axis=1, keepdims=True)
        taps_peak = jnp.max(jnp.abs(taps), axis=1, keepdims=True)
        edge = (
            jnp.where(lane < 2, key, zero)
            + pltpu.roll(jnp.where(lane < 2, value, zero), 2, axis=1)
            + pltpu.roll(key_beyond, 4, axis=1)
            + pltpu.roll(value_beyond, 6, axis=1)
            + pltpu.roll(query_beyond, 10, axis=1)
        )
        edge = jnp.where(lane == 8, gated_peak, jnp.where(lane == 9, taps_peak, edge))
        edge_rows[pl.ds(row, chunk), :] = edge
        owners = pl.ds(i * 8, 8)
        gate_src[owners] = coded(gated, gated_peak).reshape(8, OWN, LANES).astype(BF16)
        filt_src[owners] = coded(taps, taps_peak).reshape(8, OWN, LANES).astype(BF16)

    wide = edge_rows[pl.ds(0, CTX, stride=OWN), :]
    for c in range(1, OWN):
        wide = wide + pltpu.roll(edge_rows[pl.ds(c, CTX, stride=OWN), :], SLOT * c, axis=1)
    edge_wide[...] = wide
    for q in range(CTX):
        edge_src[q] = edge_wide[q : q + 1, :]

    pl.semaphore_wait(barrier, CTX - 1 + SHARE - 1)

    filt_home = filt_dst.at[me % SHARE, me // SHARE]

    def send_filter(index, carry):
        peer = index * SHARE + group

        @pl.when(peer != me)
        def _():
            remote(filt_src.at[peer], filt_home, sent.at[FILT], direct.at[me // SHARE], ctx=peer).start()

        @pl.when(peer == me)
        def _():
            pltpu.make_async_copy(filt_src.at[me], filt_home, direct.at[me // SHARE]).start()

        return carry

    lax.fori_loop(0, CTX // SHARE, send_filter, 0)

    def send_gated(peer):
        remote(gate_src.at[peer], gate_dst.at[me], sent.at[GATE], landed.at[GATE], ctx=peer).start()
        remote(edge_src.at[peer], edge_dst.at[me], sent.at[EDGE], landed.at[EDGE], ctx=peer).start()

    each_peer(send_gated)
    pltpu.make_async_copy(gate_src.at[me], gate_dst.at[me], landed.at[GATE]).start()
    pltpu.make_async_copy(edge_src.at[me], edge_dst.at[me], landed.at[EDGE]).start()
    tail = remote(edge_src, query_tail, sent.at[TAIL], landed.at[TAIL], ctx=(me + 1) % CTX)
    tail.start()

    def pass_on(index, carry):
        slot = (me // SHARE + farthest_first(CTX // SHARE - 1 - index, CTX // SHARE)) % (CTX // SHARE)
        block = filt_dst.at[group, slot]
        wait_bytes(block, direct.at[slot])
        for step in range(1, SHARE):
            peer = (part_at + step) % SHARE
            remote(block, block, sent.at[SIDE], landed.at[SIDE + step], dp=peer).start()
        return carry

    lax.fori_loop(0, CTX // SHARE, pass_on, 0)
    share = filt_dst.at[group]

    turn_re, turn_im = turn[:CTX], turn[CTX:]
    lane = lane_of((CTX, LANES))
    row_of = lax.broadcasted_iota(jnp.int32, (CTX, LANES), 0)
    wait_bytes(gate_dst, landed.at[GATE])
    for i in range(8):
        part = decoded(gate_dst[pl.ds(i * 8, 8)].astype(F32))
        plane[pl.ds(i * chunk, chunk), :] = part.reshape(chunk, LANES)
    wait_bytes(edge_dst, landed.at[EDGE])
    for p in range(CTX):
        edge_wide[p : p + 1, :] = edge_dst[p]
    edge = edge_wide[...]
    before = jnp.where(row_of >= 1, pltpu.roll(edge, 1, axis=0), 0.0)
    whole = edge + pltpu.roll(before, LANES - 4, axis=1)
    first = whole * pltpu.roll(whole, LANES - 2, axis=1)
    blocks = []
    for c in range(OWN):
        at = SLOT * c
        block = plane[pl.ds(c, CTX, stride=OWN), :] * edge[:, at + 8 : at + 9]
        block = jnp.where(lane == 0, first[:, at : at + 1], block)
        blocks.append(jnp.where(lane == 1, first[:, at + 1 : at + 2], block))
    seen = spectrum(blocks, fwd_across[...], fwd_inner[...], turn_re, turn_im)

    for step in range(1, SHARE):
        wait_bytes(filt_dst.at[(group - step) % SHARE], landed.at[SIDE + step])
    for part in range(SHARE):
        value = decoded(filt_dst[part].astype(F32))
        for k in range(CTX // SHARE):
            plane_h[pl.ds((k * SHARE + part) * OWN, OWN), :] = value[k]
    taps = [plane_h[pl.ds(c, CTX, stride=OWN), :] * edge[:, SLOT * c + 9 : SLOT * c + 10] for c in range(OWN)]
    response = spectrum(taps, fwd_across[...], fwd_inner[...], turn_re, turn_im)
    s_re, s_im = seen[:, :LANES], seen[:, LANES:]
    r_re, r_im = response[:, :LANES], response[:, LANES:]
    product = jnp.concatenate([s_re * r_re - s_im * r_im, s_re * r_im + s_im * r_re], axis=1)
    result = inverse(product, inv_across[...], inv_inner[...], turn_re, turn_im)

    peaks = jnp.zeros((CTX, LANES), F32)
    for c in range(OWN):
        part = result[:, c * LANES : (c + 1) * LANES] + skip[me * OWN + c] * blocks[c]
        peak = jnp.max(jnp.abs(part), axis=1, keepdims=True)
        peaks = jnp.where(lane == c, peak, peaks)
        plane[pl.ds(c, CTX, stride=OWN), :] = coded(part, peak)
    edge_wide[...] = peaks
    for q in range(CTX):
        peak_src[q] = edge_wide[q : q + 1, :]
    for i in range(8):
        conv_src[pl.ds(i * 8, 8)] = plane[pl.ds(i * chunk, chunk), :].reshape(8, OWN, LANES).astype(BF16)

    def send_result(peer):
        remote(conv_src.at[peer], conv_dst.at[me], sent.at[CONV], landed.at[CONV], ctx=peer).start()
        remote(peak_src.at[peer], peak_dst.at[me], sent.at[PEAK], landed.at[PEAK], ctx=peer).start()

    each_peer(send_result)
    pltpu.make_async_copy(conv_src.at[me], conv_dst.at[me], landed.at[CONV]).start()
    pltpu.make_async_copy(peak_src.at[me], peak_dst.at[me], landed.at[PEAK]).start()

    tail.wait_recv()
    shape = (8, OWN, LANES)
    lane = lane_of(shape)
    row_of = lax.broadcasted_iota(jnp.int32, shape, 1)
    keep = jnp.where(me > 0, 1.0, 0.0)
    for i in range(count // chunk):
        rows = pl.ds(i * chunk, chunk)
        behind = jnp.broadcast_to(query_tail[pl.ds(i * 8, 8)], shape) * keep
        added = jnp.zeros(shape, F32)
        for at in range(2):
            spill = jnp.sum(jnp.where(lane == row_of * SLOT + 10 + at, behind, 0.0), axis=2, keepdims=True)
            added = added + jnp.where(lane == at, spill, 0.0)
        query_part[rows, :] = query_part[rows, :] + added.reshape(chunk, LANES)

    wait_bytes(conv_dst, landed.at[CONV])
    wait_bytes(peak_dst, landed.at[PEAK])
    mine = lane == row_of
    for i in range(8):
        rows = pl.ds(i * chunk, chunk)
        peak = jnp.broadcast_to(peak_dst[pl.ds(i * 8, 8)], shape)
        peak = jnp.sum(jnp.where(mine, peak, 0.0), axis=2, keepdims=True)
        part = decoded(conv_dst[pl.ds(i * 8, 8)].astype(F32)) * peak
        out_ref[rows, :] = query_part[rows, :] * part.reshape(chunk, LANES)

    others = pl.ds(0, CTX - 1)
    for slot, source in ((GATE, gate_src), (EDGE, edge_src), (CONV, conv_src), (PEAK, peak_src)):
        wait_bytes(source.at[others], sent.at[slot])

    own_group = (2 * me - part_at) % SHARE == 0

    @pl.when(own_group)
    def _():
        wait_bytes(filt_src.at[pl.ds(0, CTX // SHARE - 1)], sent.at[FILT])

    @pl.when(jnp.logical_not(own_group))
    def _():
        wait_bytes(filt_src.at[pl.ds(0, CTX // SHARE)], sent.at[FILT])

    for _ in range(1, SHARE):
        wait_bytes(share, sent.at[SIDE])
    tail.wait_send()


def halves(table):
    high = table.astype(jnp.bfloat16)
    return high, (table - high.astype(np.float64)).astype(jnp.bfloat16)


def tables():
    points = 2 * CTX * LANES
    j, s, k1, k2 = np.arange(CTX), np.arange(LANES), np.arange(CTX) + 0.5, np.arange(LANES)
    outer = 2 * math.pi / LANES * np.outer(k1, j)
    high, low = halves(np.concatenate([np.cos(outer), -np.sin(outer)], axis=0))
    fwd_across = np.concatenate([high, high, low, low], axis=1)
    high, low = halves(np.concatenate([np.cos(outer.T), -np.sin(outer.T)], axis=1) * (2.0 / points))
    inv_across = np.concatenate([high, high, low], axis=1)
    inner = 2 * math.pi / LANES * (np.outer(s, k2) % LANES)
    cos, sin = np.cos(inner), np.sin(inner)
    high, low = halves(np.block([[cos, -sin], [sin, cos]]))
    fwd_inner = np.concatenate([high, high, low], axis=0)
    high, low = halves(np.block([[cos, sin], [-sin, cos]]))
    inv_inner = np.concatenate([high, high, low], axis=0)
    angle = 2 * math.pi / points * np.outer(k1, s)
    turn = np.concatenate([np.cos(angle), -np.sin(angle)], axis=0).astype(np.float32)
    return fwd_across, fwd_inner, inv_inner, inv_across, turn


def solution(mesh):
    constants = tables()

    def body(features_in, short_weight, long_filter, skip_gain):
        operands = (features_in, short_weight.T, long_filter, skip_gain, *map(jnp.asarray, constants))
        count = long_filter.shape[0]
        rows = (CTX, OWN, LANES)
        row = (CTX, 1, LANES)
        own_copies = [
            (pltpu.SMEM if value.ndim == 1 else pltpu.VMEM)(value.shape, value.dtype) for value in operands
        ]
        scratch = own_copies + [
            pltpu.VMEM((3 * count, 8), F32),
            pltpu.VMEM((count, LANES), F32),
            pltpu.VMEM((CTX, LANES), F32),
            pltpu.VMEM((count, LANES), F32),
            pltpu.VMEM((count, LANES), F32),
            pltpu.VMEM((count, LANES), F32),
            pltpu.VMEM(rows, BF16), pltpu.VMEM(row, F32), pltpu.VMEM(rows, BF16),
            pltpu.VMEM(rows, BF16), pltpu.VMEM(row, F32), pltpu.VMEM((SHARE, CTX // SHARE, OWN, LANES), BF16),
            pltpu.VMEM(rows, BF16), pltpu.VMEM(row, F32),
            pltpu.VMEM(rows, BF16), pltpu.VMEM(row, F32),
            pltpu.VMEM(row, F32),
            pltpu.SemaphoreType.DMA((len(operands),)),
            pltpu.SemaphoreType.DMA((SLOTS,)),
            pltpu.SemaphoreType.DMA((SLOTS,)),
            pltpu.SemaphoreType.DMA((CTX // SHARE,)),
        ]
        operands = [pltpu.with_memory_space_constraint(value, pltpu.HBM) for value in operands]
        return pl.pallas_call(
            kernel,
            out_shape=jax.ShapeDtypeStruct((count, LANES), F32),
            in_specs=[pl.BlockSpec(memory_space=pltpu.HBM)] * len(operands),
            out_specs=pl.BlockSpec(memory_space=pltpu.VMEM),
            scratch_shapes=scratch,
            compiler_params=pltpu.CompilerParams(
                collective_id=0, has_side_effects=True, vmem_limit_bytes=48 * 1024 * 1024
            ),
        )(*operands)

    return jax.shard_map(
        body,
        mesh=mesh,
        in_specs=(P(None, ("dp", "ctx")), P(), P(None, "ctx"), P()),
        out_specs=P(None, ("dp", "ctx")),
        check_vma=False,
    )
```

```python
import functools
import math

import jax
import jax.numpy as jnp
import numpy as np
from jax import lax
from jax.experimental import pallas as pl
from jax.experimental.pallas import tpu as pltpu
from jax.sharding import PartitionSpec as P

MESH = pl.DeviceIdType.MESH
F32, BF16 = jnp.float32, jnp.bfloat16
RINGS = (16, 4)
CTX = RINGS[0] * RINGS[1]
SHARE = 8
LANES = 128
OWN = 8
LIFT = 2.0**7.5
SLOT = 16


def coded(value, largest):
    ratio = jnp.where(largest > 1e-30, LIFT / jnp.maximum(largest, 1e-30), 0.0)
    power = value * ratio
    for _ in range(4):
        power = power * power
    return jnp.where(value < 0, -power, power)


def decoded(code):
    size = jnp.abs(code)
    root = jnp.exp(jnp.log(jnp.maximum(size, 1e-37)) * (1.0 / 16.0)) * (1.0 / LIFT)
    root = jnp.where(size > 1e-37, root, 0.0)
    return jnp.where(code < 0, -root, root)


def farthest_first(index, extent):
    step = (index + 1) // 2
    return jnp.where(lax.rem(index, 2) == 0, extent // 2 + step, extent // 2 - step)


def each_peer(visit, begin=0):
    me = lax.axis_index("ctx")
    at_z, at_x = lax.div(me, RINGS[1]), lax.rem(me, RINGS[1])
    to_x = [lax.rem(at_x + step, RINGS[1]) for step in (2, 1, 3)]

    def plane(index, carry):
        step = lax.rem(index + begin, RINGS[0])
        step = lax.rem(at_z + farthest_first(step, RINGS[0]), RINGS[0])
        row = step * RINGS[1]
        for x in to_x:
            visit(row + x)

        @pl.when(step != at_z)
        def _():
            visit(row + at_x)

        return carry

    lax.fori_loop(0, RINGS[0], plane, 0)


def remote(source, target, sent, landed, **where):
    return pltpu.make_async_remote_copy(
        src_ref=source, dst_ref=target, send_sem=sent, recv_sem=landed, device_id=where, device_id_type=MESH
    )


def wait_bytes(ref, semaphore):
    pltpu.make_async_copy(ref, ref, semaphore).wait()


def split(value):
    high = value.astype(BF16)
    return high, (value - high.astype(F32)).astype(BF16)


def spectrum(blocks, across, inner, turn_re, turn_im):
    high, low = split(jnp.concatenate(blocks, axis=1))
    outer = jnp.dot(across, jnp.concatenate([high, low, high, low], axis=0), preferred_element_type=F32)
    rows = []
    for c in range(OWN):
        part = outer[:, c * LANES : (c + 1) * LANES]
        re, im = part[:CTX], part[CTX:]
        rows.append(jnp.concatenate([re * turn_re - im * turn_im, re * turn_im + im * turn_re], axis=1))
    high, low = split(jnp.concatenate(rows, axis=0))
    return jnp.dot(jnp.concatenate([high, low, high], axis=1), inner, preferred_element_type=F32)


def inverse(product, across, inner, turn_re, turn_im):
    high, low = split(product)
    mixed = jnp.dot(jnp.concatenate([high, low, high], axis=1), inner, preferred_element_type=F32)
    columns = []
    for c in range(OWN):
        part = mixed[c * CTX : (c + 1) * CTX]
        re, im = part[:, :LANES], part[:, LANES:]
        columns.append(jnp.concatenate([re * turn_re + im * turn_im, im * turn_re - re * turn_im], axis=0))
    high, low = split(jnp.concatenate(columns, axis=1))
    return jnp.dot(across, jnp.concatenate([high, low, high], axis=0), preferred_element_type=F32)


def lane_of(shape):
    return lax.broadcasted_iota(jnp.int32, shape, len(shape) - 1)


GATE, EDGE, FILT, CONV, PEAK, TAIL, SIDE, SLOTS = 0, 1, 2, 3, 4, 5, 6, 6 + SHARE


def kernel(
    feat_hbm, short_hbm, filt_hbm, skip_hbm, fwd_across_hbm, fwd_inner_hbm, inv_inner_hbm, inv_across_hbm, turn_hbm,
    out_ref,
    feat, short_flat, filt, skip, fwd_across, fwd_inner, inv_inner, inv_across, turn,
    short, edge_rows, edge_wide, plane, plane_h, query_part,
    gate_src, edge_src, filt_src, gate_dst, edge_dst, filt_dst,
    conv_src, peak_src, conv_dst, peak_dst, query_tail,
    load_sem, sent, landed, direct,
):
    me, part_at = lax.axis_index("ctx"), lax.axis_index("dp")
    member = lax.rem(part_at, SHARE)
    group = lax.rem(member - lax.rem(me, SHARE) + SHARE, SHARE)
    others = [part_at - member + lax.rem(member + step, SHARE) for step in range(1, SHARE)]
    barrier = pltpu.get_barrier_semaphore()
    each_peer(lambda peer: pl.semaphore_signal(barrier, inc=1, device_id={"ctx": peer}, device_id_type=MESH))
    for peer in others:
        pl.semaphore_signal(barrier, inc=1, device_id={"dp": peer}, device_id_type=MESH)

    pairs = (
        (feat_hbm, feat), (short_hbm, short_flat), (filt_hbm, filt), (skip_hbm, skip), (fwd_across_hbm, fwd_across),
        (fwd_inner_hbm, fwd_inner), (inv_inner_hbm, inv_inner), (inv_across_hbm, inv_across), (turn_hbm, turn),
    )
    loads = [pltpu.make_async_copy(source, target, load_sem.at[i]) for i, (source, target) in enumerate(pairs)]
    for load in loads:
        load.start()
    for load in loads:
        load.wait()

    count = OWN * CTX
    chunk = 8 * OWN
    lane = lane_of((chunk, LANES))
    for i in range(3 * count // LANES):
        taps = jnp.concatenate([short_flat[:, i * LANES : (i + 1) * LANES], jnp.zeros((5, LANES), F32)], axis=0)
        short[pl.ds(i * LANES, LANES), :] = taps.T

    def local_feature(row):
        rows = pl.ds(row, chunk)
        value = feat[rows, :].astype(F32)
        taps = short[rows, :]
        once, twice = pltpu.roll(value, 1, axis=1), pltpu.roll(value, 2, axis=1)
        near = taps[:, 1:2] * once
        far = taps[:, 2:3] * twice
        zero = jnp.zeros_like(value)
        inside = taps[:, 0:1] * value + jnp.where(lane >= 1, near, zero) + jnp.where(lane >= 2, far, zero)
        beyond = jnp.where(lane < 1, near, zero) + jnp.where(lane < 2, far, zero)
        return inside, beyond

    for i in range(count // chunk):
        row = i * chunk
        zero = jnp.zeros((chunk, LANES), F32)
        query, query_beyond = local_feature(row)
        query_part[pl.ds(row, chunk), :] = query
        key, key_beyond = local_feature(count + row)
        value, value_beyond = local_feature(2 * count + row)
        gated = key * value
        gated = jnp.where(lane >= 2, gated, zero)
        taps = filt[pl.ds(row, chunk), :]
        gated_peak = jnp.max(jnp.abs(gated), axis=1, keepdims=True)
        taps_peak = jnp.max(jnp.abs(taps), axis=1, keepdims=True)
        edge = (
            jnp.where(lane < 2, key, zero)
            + pltpu.roll(jnp.where(lane < 2, value, zero), 2, axis=1)
            + pltpu.roll(key_beyond, 4, axis=1)
            + pltpu.roll(value_beyond, 6, axis=1)
            + pltpu.roll(query_beyond, 10, axis=1)
        )
        edge = jnp.where(lane == 8, gated_peak, jnp.where(lane == 9, taps_peak, edge))
        edge_rows[pl.ds(row, chunk), :] = edge
        owners = pl.ds(i * 8, 8)
        gate_src[owners] = coded(gated, gated_peak).reshape(8, OWN, LANES).astype(BF16)
        filt_src[owners] = coded(taps, taps_peak).reshape(8, OWN, LANES).astype(BF16)

    wide = edge_rows[pl.ds(0, CTX, stride=OWN), :]
    for c in range(1, OWN):
        wide = wide + pltpu.roll(edge_rows[pl.ds(c, CTX, stride=OWN), :], SLOT * c, axis=1)
    edge_wide[...] = wide
    for q in range(CTX):
        edge_src[q] = edge_wide[q : q + 1, :]

    pl.semaphore_wait(barrier, CTX - 1 + SHARE - 1)

    filt_home = filt_dst.at[me % SHARE, me // SHARE]

    def send_filter(index, carry):
        place = lax.rem(me // SHARE + farthest_first(index, CTX // SHARE), CTX // SHARE)
        peer = place * SHARE + group

        @pl.when(peer != me)
        def _():
            remote(filt_src.at[peer], filt_home, sent.at[FILT], direct.at[me // SHARE], ctx=peer).start()

        @pl.when(peer == me)
        def _():
            pltpu.make_async_copy(filt_src.at[me], filt_home, direct.at[me // SHARE]).start()

        return carry

    lax.fori_loop(0, CTX // SHARE, send_filter, 0)

    def send_gated(peer):
        remote(gate_src.at[peer], gate_dst.at[me], sent.at[GATE], landed.at[GATE], ctx=peer).start()
        remote(edge_src.at[peer], edge_dst.at[me], sent.at[EDGE], landed.at[EDGE], ctx=peer).start()

    each_peer(send_gated, jnp.where(me < 4 * RINGS[1], 0, 7))
    pltpu.make_async_copy(gate_src.at[me], gate_dst.at[me], landed.at[GATE]).start()
    pltpu.make_async_copy(edge_src.at[me], edge_dst.at[me], landed.at[EDGE]).start()
    tail = remote(edge_src, query_tail, sent.at[TAIL], landed.at[TAIL], ctx=(me + 1) % CTX)
    tail.start()

    my_slot = me // SHARE

    def pass_on(index, carry):
        slot = lax.rem(my_slot + farthest_first(CTX // SHARE - 1 - index, CTX // SHARE), CTX // SHARE)
        block = filt_dst.at[group, slot]
        wait_bytes(block, direct.at[slot])
        for step, peer in enumerate(others):
            remote(block, block, sent.at[SIDE], landed.at[SIDE + 1 + step], dp=peer).start()
        return carry

    lax.fori_loop(0, CTX // SHARE, pass_on, 0)
    share = filt_dst.at[group]

    turn_re, turn_im = turn[:CTX], turn[CTX:]
    lane = lane_of((CTX, LANES))
    row_of = lax.broadcasted_iota(jnp.int32, (CTX, LANES), 0)
    wait_bytes(gate_dst, landed.at[GATE])
    for i in range(8):
        part = decoded(gate_dst[pl.ds(i * 8, 8)].astype(F32))
        plane[pl.ds(i * chunk, chunk), :] = part.reshape(chunk, LANES)
    wait_bytes(edge_dst, landed.at[EDGE])
    for p in range(CTX):
        edge_wide[p : p + 1, :] = edge_dst[p]
    edge = edge_wide[...]
    before = jnp.where(row_of >= 1, pltpu.roll(edge, 1, axis=0), 0.0)
    whole = edge + pltpu.roll(before, LANES - 4, axis=1)
    first = whole * pltpu.roll(whole, LANES - 2, axis=1)
    blocks = []
    for c in range(OWN):
        at = SLOT * c
        block = plane[pl.ds(c, CTX, stride=OWN), :] * edge[:, at + 8 : at + 9]
        block = jnp.where(lane == 0, first[:, at : at + 1], block)
        blocks.append(jnp.where(lane == 1, first[:, at + 1 : at + 2], block))
    seen = spectrum(blocks, fwd_across[...], fwd_inner[...], turn_re, turn_im)

    for step in range(1, SHARE):
        wait_bytes(filt_dst.at[(group - step) % SHARE], landed.at[SIDE + step])
    for part in range(SHARE):
        value = decoded(filt_dst[part].astype(F32))
        for k in range(CTX // SHARE):
            plane_h[pl.ds((k * SHARE + part) * OWN, OWN), :] = value[k]
    taps = [plane_h[pl.ds(c, CTX, stride=OWN), :] * edge[:, SLOT * c + 9 : SLOT * c + 10] for c in range(OWN)]
    response = spectrum(taps, fwd_across[...], fwd_inner[...], turn_re, turn_im)
    s_re, s_im = seen[:, :LANES], seen[:, LANES:]
    r_re, r_im = response[:, :LANES], response[:, LANES:]
    product = jnp.concatenate([s_re * r_re - s_im * r_im, s_re * r_im + s_im * r_re], axis=1)
    result = inverse(product, inv_across[...], inv_inner[...], turn_re, turn_im)

    peaks = jnp.zeros((CTX, LANES), F32)
    for c in range(OWN):
        part = result[:, c * LANES : (c + 1) * LANES] + skip[me * OWN + c] * blocks[c]
        peak = jnp.max(jnp.abs(part), axis=1, keepdims=True)
        peaks = jnp.where(lane == c, peak, peaks)
        plane[pl.ds(c, CTX, stride=OWN), :] = coded(part, peak)
    edge_wide[...] = peaks
    for q in range(CTX):
        peak_src[q] = edge_wide[q : q + 1, :]
    for i in range(8):
        conv_src[pl.ds(i * 8, 8)] = plane[pl.ds(i * chunk, chunk), :].reshape(8, OWN, LANES).astype(BF16)

    def send_result(peer):
        remote(conv_src.at[peer], conv_dst.at[me], sent.at[CONV], landed.at[CONV], ctx=peer).start()
        remote(peak_src.at[peer], peak_dst.at[me], sent.at[PEAK], landed.at[PEAK], ctx=peer).start()

    each_peer(send_result)
    pltpu.make_async_copy(conv_src.at[me], conv_dst.at[me], landed.at[CONV]).start()
    pltpu.make_async_copy(peak_src.at[me], peak_dst.at[me], landed.at[PEAK]).start()

    tail.wait_recv()
    shape = (8, OWN, LANES)
    lane = lane_of(shape)
    row_of = lax.broadcasted_iota(jnp.int32, shape, 1)
    keep = jnp.where(me > 0, 1.0, 0.0)
    for i in range(count // chunk):
        rows = pl.ds(i * chunk, chunk)
        behind = jnp.broadcast_to(query_tail[pl.ds(i * 8, 8)], shape) * keep
        added = jnp.zeros(shape, F32)
        for at in range(2):
            spill = jnp.sum(jnp.where(lane == row_of * SLOT + 10 + at, behind, 0.0), axis=2, keepdims=True)
            added = added + jnp.where(lane == at, spill, 0.0)
        query_part[rows, :] = query_part[rows, :] + added.reshape(chunk, LANES)

    wait_bytes(conv_dst, landed.at[CONV])
    wait_bytes(peak_dst, landed.at[PEAK])
    mine = lane == row_of
    for i in range(8):
        rows = pl.ds(i * chunk, chunk)
        peak = jnp.broadcast_to(peak_dst[pl.ds(i * 8, 8)], shape)
        peak = jnp.sum(jnp.where(mine, peak, 0.0), axis=2, keepdims=True)
        part = decoded(conv_dst[pl.ds(i * 8, 8)].astype(F32)) * peak
        out_ref[rows, :] = query_part[rows, :] * part.reshape(chunk, LANES)

    away = pl.ds(0, CTX - 1)
    for slot, source in ((GATE, gate_src), (EDGE, edge_src), (CONV, conv_src), (PEAK, peak_src)):
        wait_bytes(source.at[away], sent.at[slot])

    own_group = group == lax.rem(me, SHARE)

    @pl.when(own_group)
    def _():
        wait_bytes(filt_src.at[pl.ds(0, CTX // SHARE - 1)], sent.at[FILT])

    @pl.when(jnp.logical_not(own_group))
    def _():
        wait_bytes(filt_src.at[pl.ds(0, CTX // SHARE)], sent.at[FILT])

    for _ in range(1, SHARE):
        wait_bytes(share, sent.at[SIDE])
    tail.wait_send()


def halves(table):
    high = table.astype(jnp.bfloat16)
    return high, (table - high.astype(np.float64)).astype(jnp.bfloat16)


def tables():
    points = 2 * CTX * LANES
    j, s, k1, k2 = np.arange(CTX), np.arange(LANES), np.arange(CTX) + 0.5, np.arange(LANES)
    outer = 2 * math.pi / LANES * np.outer(k1, j)
    high, low = halves(np.concatenate([np.cos(outer), -np.sin(outer)], axis=0))
    fwd_across = np.concatenate([high, high, low, low], axis=1)
    high, low = halves(np.concatenate([np.cos(outer.T), -np.sin(outer.T)], axis=1) * (2.0 / points))
    inv_across = np.concatenate([high, high, low], axis=1)
    inner = 2 * math.pi / LANES * (np.outer(s, k2) % LANES)
    cos, sin = np.cos(inner), np.sin(inner)
    high, low = halves(np.block([[cos, -sin], [sin, cos]]))
    fwd_inner = np.concatenate([high, high, low], axis=0)
    high, low = halves(np.block([[cos, sin], [-sin, cos]]))
    inv_inner = np.concatenate([high, high, low], axis=0)
    angle = 2 * math.pi / points * np.outer(k1, s)
    turn = np.concatenate([np.cos(angle), -np.sin(angle)], axis=0).astype(np.float32)
    return fwd_across, fwd_inner, inv_inner, inv_across, turn


def solution(mesh):
    constants = tables()

    def body(features_in, short_weight, long_filter, skip_gain):
        operands = (features_in, short_weight.T, long_filter, skip_gain, *map(jnp.asarray, constants))
        count = long_filter.shape[0]
        rows = (CTX, OWN, LANES)
        row = (CTX, 1, LANES)
        own_copies = [
            (pltpu.SMEM if value.ndim == 1 else pltpu.VMEM)(value.shape, value.dtype) for value in operands
        ]
        scratch = own_copies + [
            pltpu.VMEM((3 * count, 8), F32),
            pltpu.VMEM((count, LANES), F32),
            pltpu.VMEM((CTX, LANES), F32),
            pltpu.VMEM((count, LANES), F32),
            pltpu.VMEM((count, LANES), F32),
            pltpu.VMEM((count, LANES), F32),
            pltpu.VMEM(rows, BF16), pltpu.VMEM(row, F32), pltpu.VMEM(rows, BF16),
            pltpu.VMEM(rows, BF16), pltpu.VMEM(row, F32), pltpu.VMEM((SHARE, CTX // SHARE, OWN, LANES), BF16),
            pltpu.VMEM(rows, BF16), pltpu.VMEM(row, F32),
            pltpu.VMEM(rows, BF16), pltpu.VMEM(row, F32),
            pltpu.VMEM(row, F32),
            pltpu.SemaphoreType.DMA((len(operands),)),
            pltpu.SemaphoreType.DMA((SLOTS,)),
            pltpu.SemaphoreType.DMA((SLOTS,)),
            pltpu.SemaphoreType.DMA((CTX // SHARE,)),
        ]
        operands = [pltpu.with_memory_space_constraint(value, pltpu.HBM) for value in operands]
        return pl.pallas_call(
            kernel,
            out_shape=jax.ShapeDtypeStruct((count, LANES), F32),
            in_specs=[pl.BlockSpec(memory_space=pltpu.HBM)] * len(operands),
            out_specs=pl.BlockSpec(memory_space=pltpu.VMEM),
            scratch_shapes=scratch,
            compiler_params=pltpu.CompilerParams(
                collective_id=0, has_side_effects=True, vmem_limit_bytes=48 * 1024 * 1024
            ),
        )(*operands)

    return jax.shard_map(
        body,
        mesh=mesh,
        in_specs=(P(None, ("dp", "ctx")), P(), P(None, "ctx"), P()),
        out_specs=P(None, ("dp", "ctx")),
        check_vma=False,
    )
```

```python
import functools
import math

import jax
import jax.numpy as jnp
import numpy as np
from jax import lax
from jax.experimental import pallas as pl
from jax.experimental.pallas import tpu as pltpu
from jax.sharding import PartitionSpec as P

MESH = pl.DeviceIdType.MESH
F32, BF16 = jnp.float32, jnp.bfloat16
RINGS = (16, 4)
CTX = RINGS[0] * RINGS[1]
SHARE = 4
LANES = 128
OWN = 8
LIFT = 2.0**7.5
SLOT = 16


def coded(value, largest):
    ratio = jnp.where(largest > 1e-30, LIFT / jnp.maximum(largest, 1e-30), 0.0)
    power = value * ratio
    for _ in range(4):
        power = power * power
    return jnp.where(value < 0, -power, power)


def decoded(code):
    size = jnp.abs(code)
    root = jnp.exp(jnp.log(jnp.maximum(size, 1e-37)) * (1.0 / 16.0)) * (1.0 / LIFT)
    root = jnp.where(size > 1e-37, root, 0.0)
    return jnp.where(code < 0, -root, root)


def farthest_first(index, extent):
    step = (index + 1) // 2
    return jnp.where(lax.rem(index, 2) == 0, extent // 2 + step, extent // 2 - step)


def each_peer(visit, begin=0):
    me = lax.axis_index("ctx")
    at_z, at_x = lax.div(me, RINGS[1]), lax.rem(me, RINGS[1])
    to_x = [lax.rem(at_x + step, RINGS[1]) for step in (2, 1, 3)]

    def plane(index, carry):
        step = lax.rem(index + begin, RINGS[0])
        step = lax.rem(at_z + farthest_first(step, RINGS[0]), RINGS[0])
        row = step * RINGS[1]
        for x in to_x:
            visit(row + x)

        @pl.when(step != at_z)
        def _():
            visit(row + at_x)

        return carry

    lax.fori_loop(0, RINGS[0], plane, 0)


def remote(source, target, sent, landed, **where):
    return pltpu.make_async_remote_copy(
        src_ref=source, dst_ref=target, send_sem=sent, recv_sem=landed, device_id=where, device_id_type=MESH
    )


def wait_bytes(ref, semaphore):
    pltpu.make_async_copy(ref, ref, semaphore).wait()


def split(value):
    high = value.astype(BF16)
    return high, (value - high.astype(F32)).astype(BF16)


def spectrum(blocks, across, inner, turn_re, turn_im):
    high, low = split(jnp.concatenate(blocks, axis=1))
    outer = jnp.dot(across, jnp.concatenate([high, low, high, low], axis=0), preferred_element_type=F32)
    rows = []
    for c in range(OWN):
        part = outer[:, c * LANES : (c + 1) * LANES]
        re, im = part[:CTX], part[CTX:]
        rows.append(jnp.concatenate([re * turn_re - im * turn_im, re * turn_im + im * turn_re], axis=1))
    high, low = split(jnp.concatenate(rows, axis=0))
    return jnp.dot(jnp.concatenate([high, low, high], axis=1), inner, preferred_element_type=F32)


def inverse(product, across, inner, turn_re, turn_im):
    high, low = split(product)
    mixed = jnp.dot(jnp.concatenate([high, low, high], axis=1), inner, preferred_element_type=F32)
    columns = []
    for c in range(OWN):
        part = mixed[c * CTX : (c + 1) * CTX]
        re, im = part[:, :LANES], part[:, LANES:]
        columns.append(jnp.concatenate([re * turn_re + im * turn_im, im * turn_re - re * turn_im], axis=0))
    high, low = split(jnp.concatenate(columns, axis=1))
    return jnp.dot(across, jnp.concatenate([high, low, high], axis=0), preferred_element_type=F32)


def lane_of(shape):
    return lax.broadcasted_iota(jnp.int32, shape, len(shape) - 1)


GATE, EDGE, FILT, CONV, PEAK, TAIL, SIDE, SLOTS = 0, 1, 2, 3, 4, 5, 6, 6 + SHARE


def kernel(
    feat_hbm, short_hbm, filt_hbm, skip_hbm, fwd_across_hbm, fwd_inner_hbm, inv_inner_hbm, inv_across_hbm, turn_hbm,
    out_ref,
    feat, short_flat, filt, skip, fwd_across, fwd_inner, inv_inner, inv_across, turn,
    short, edge_rows, edge_wide, plane, plane_h, query_part,
    gate_src, edge_src, filt_src, gate_dst, edge_dst, filt_dst,
    conv_src, peak_src, conv_dst, peak_dst, query_tail,
    load_sem, sent, landed, direct,
):
    me, part_at = lax.axis_index("ctx"), lax.axis_index("dp")
    member = lax.rem(part_at, SHARE)
    group = lax.rem(member - lax.rem(me, SHARE) + SHARE, SHARE)
    others = [part_at - member + lax.rem(member + step, SHARE) for step in range(1, SHARE)]
    barrier = pltpu.get_barrier_semaphore()
    each_peer(lambda peer: pl.semaphore_signal(barrier, inc=1, device_id={"ctx": peer}, device_id_type=MESH))
    for peer in others:
        pl.semaphore_signal(barrier, inc=1, device_id={"dp": peer}, device_id_type=MESH)

    pairs = (
        (feat_hbm, feat), (short_hbm, short_flat), (filt_hbm, filt), (skip_hbm, skip), (fwd_across_hbm, fwd_across),
        (fwd_inner_hbm, fwd_inner), (inv_inner_hbm, inv_inner), (inv_across_hbm, inv_across), (turn_hbm, turn),
    )
    loads = [pltpu.make_async_copy(source, target, load_sem.at[i]) for i, (source, target) in enumerate(pairs)]
    for load in loads:
        load.start()
    for load in loads:
        load.wait()

    count = OWN * CTX
    chunk = 8 * OWN
    lane = lane_of((chunk, LANES))
    for i in range(3 * count // LANES):
        taps = jnp.concatenate([short_flat[:, i * LANES : (i + 1) * LANES], jnp.zeros((5, LANES), F32)], axis=0)
        short[pl.ds(i * LANES, LANES), :] = taps.T

    def local_feature(row):
        rows = pl.ds(row, chunk)
        value = feat[rows, :].astype(F32)
        taps = short[rows, :]
        once, twice = pltpu.roll(value, 1, axis=1), pltpu.roll(value, 2, axis=1)
        near = taps[:, 1:2] * once
        far = taps[:, 2:3] * twice
        zero = jnp.zeros_like(value)
        inside = taps[:, 0:1] * value + jnp.where(lane >= 1, near, zero) + jnp.where(lane >= 2, far, zero)
        beyond = jnp.where(lane < 1, near, zero) + jnp.where(lane < 2, far, zero)
        return inside, beyond

    for i in range(count // chunk):
        row = i * chunk
        zero = jnp.zeros((chunk, LANES), F32)
        query, query_beyond = local_feature(row)
        query_part[pl.ds(row, chunk), :] = query
        key, key_beyond = local_feature(count + row)
        value, value_beyond = local_feature(2 * count + row)
        gated = key * value
        gated = jnp.where(lane >= 2, gated, zero)
        taps = filt[pl.ds(row, chunk), :]
        gated_peak = jnp.max(jnp.abs(gated), axis=1, keepdims=True)
        taps_peak = jnp.max(jnp.abs(taps), axis=1, keepdims=True)
        edge = (
            jnp.where(lane < 2, key, zero)
            + pltpu.roll(jnp.where(lane < 2, value, zero), 2, axis=1)
            + pltpu.roll(key_beyond, 4, axis=1)
            + pltpu.roll(value_beyond, 6, axis=1)
            + pltpu.roll(query_beyond, 10, axis=1)
        )
        edge = jnp.where(lane == 8, gated_peak, jnp.where(lane == 9, taps_peak, edge))
        edge_rows[pl.ds(row, chunk), :] = edge
        owners = pl.ds(i * 8, 8)
        gate_src[owners] = coded(gated, gated_peak).reshape(8, OWN, LANES).astype(BF16)
        filt_src[owners] = coded(taps, taps_peak).reshape(8, OWN, LANES).astype(BF16)

    wide = edge_rows[pl.ds(0, CTX, stride=OWN), :]
    for c in range(1, OWN):
        wide = wide + pltpu.roll(edge_rows[pl.ds(c, CTX, stride=OWN), :], SLOT * c, axis=1)
    edge_wide[...] = wide
    for q in range(CTX):
        edge_src[q] = edge_wide[q : q + 1, :]

    pl.semaphore_wait(barrier, CTX - 1 + SHARE - 1)

    filt_home = filt_dst.at[me % SHARE, me // SHARE]

    def send_filter(index, carry):
        place = lax.rem(me // SHARE + farthest_first(index, CTX // SHARE), CTX // SHARE)
        peer = place * SHARE + group

        @pl.when(peer != me)
        def _():
            remote(filt_src.at[peer], filt_home, sent.at[FILT], direct.at[me // SHARE], ctx=peer).start()

        @pl.when(peer == me)
        def _():
            pltpu.make_async_copy(filt_src.at[me], filt_home, direct.at[me // SHARE]).start()

        return carry

    lax.fori_loop(0, CTX // SHARE, send_filter, 0)

    def send_gated(peer):
        remote(gate_src.at[peer], gate_dst.at[me], sent.at[GATE], landed.at[GATE], ctx=peer).start()
        remote(edge_src.at[peer], edge_dst.at[me], sent.at[EDGE], landed.at[EDGE], ctx=peer).start()

    each_peer(send_gated, jnp.where(me < 2 * RINGS[1], 0, 7))
    pltpu.make_async_copy(gate_src.at[me], gate_dst.at[me], landed.at[GATE]).start()
    pltpu.make_async_copy(edge_src.at[me], edge_dst.at[me], landed.at[EDGE]).start()
    tail = remote(edge_src, query_tail, sent.at[TAIL], landed.at[TAIL], ctx=(me + 1) % CTX)
    tail.start()

    my_slot = me // SHARE

    def pass_on(index, carry):
        slot = lax.rem(my_slot + farthest_first(CTX // SHARE - 1 - index, CTX // SHARE), CTX // SHARE)
        block = filt_dst.at[group, slot]
        wait_bytes(block, direct.at[slot])
        for step, peer in enumerate(others):
            remote(block, block, sent.at[SIDE], landed.at[SIDE + 1 + step], dp=peer).start()
        return carry

    lax.fori_loop(0, CTX // SHARE, pass_on, 0)
    share = filt_dst.at[group]

    turn_re, turn_im = turn[:CTX], turn[CTX:]
    lane = lane_of((CTX, LANES))
    row_of = lax.broadcasted_iota(jnp.int32, (CTX, LANES), 0)
    wait_bytes(gate_dst, landed.at[GATE])
    for i in range(8):
        part = decoded(gate_dst[pl.ds(i * 8, 8)].astype(F32))
        plane[pl.ds(i * chunk, chunk), :] = part.reshape(chunk, LANES)
    wait_bytes(edge_dst, landed.at[EDGE])
    for p in range(CTX):
        edge_wide[p : p + 1, :] = edge_dst[p]
    edge = edge_wide[...]
    before = jnp.where(row_of >= 1, pltpu.roll(edge, 1, axis=0), 0.0)
    whole = edge + pltpu.roll(before, LANES - 4, axis=1)
    first = whole * pltpu.roll(whole, LANES - 2, axis=1)
    blocks = []
    for c in range(OWN):
        at = SLOT * c
        block = plane[pl.ds(c, CTX, stride=OWN), :] * edge[:, at + 8 : at + 9]
        block = jnp.where(lane == 0, first[:, at : at + 1], block)
        blocks.append(jnp.where(lane == 1, first[:, at + 1 : at + 2], block))
    seen = spectrum(blocks, fwd_across[...], fwd_inner[...], turn_re, turn_im)

    for step in range(1, SHARE):
        wait_bytes(filt_dst.at[(group - step) % SHARE], landed.at[SIDE + step])
    for part in range(SHARE):
        value = decoded(filt_dst[part].astype(F32))
        for k in range(CTX // SHARE):
            plane_h[pl.ds((k * SHARE + part) * OWN, OWN), :] = value[k]
    taps = [plane_h[pl.ds(c, CTX, stride=OWN), :] * edge[:, SLOT * c + 9 : SLOT * c + 10] for c in range(OWN)]
    response = spectrum(taps, fwd_across[...], fwd_inner[...], turn_re, turn_im)
    s_re, s_im = seen[:, :LANES], seen[:, LANES:]
    r_re, r_im = response[:, :LANES], response[:, LANES:]
    product = jnp.concatenate([s_re * r_re - s_im * r_im, s_re * r_im + s_im * r_re], axis=1)
    result = inverse(product, inv_across[...], inv_inner[...], turn_re, turn_im)

    peaks = jnp.zeros((CTX, LANES), F32)
    for c in range(OWN):
        part = result[:, c * LANES : (c + 1) * LANES] + skip[me * OWN + c] * blocks[c]
        peak = jnp.max(jnp.abs(part), axis=1, keepdims=True)
        peaks = jnp.where(lane == c, peak, peaks)
        plane[pl.ds(c, CTX, stride=OWN), :] = coded(part, peak)
    edge_wide[...] = peaks
    for q in range(CTX):
        peak_src[q] = edge_wide[q : q + 1, :]
    for i in range(8):
        conv_src[pl.ds(i * 8, 8)] = plane[pl.ds(i * chunk, chunk), :].reshape(8, OWN, LANES).astype(BF16)

    def send_result(peer):
        remote(conv_src.at[peer], conv_dst.at[me], sent.at[CONV], landed.at[CONV], ctx=peer).start()
        remote(peak_src.at[peer], peak_dst.at[me], sent.at[PEAK], landed.at[PEAK], ctx=peer).start()

    each_peer(send_result)
    pltpu.make_async_copy(conv_src.at[me], conv_dst.at[me], landed.at[CONV]).start()
    pltpu.make_async_copy(peak_src.at[me], peak_dst.at[me], landed.at[PEAK]).start()

    tail.wait_recv()
    shape = (8, OWN, LANES)
    lane = lane_of(shape)
    row_of = lax.broadcasted_iota(jnp.int32, shape, 1)
    keep = jnp.where(me > 0, 1.0, 0.0)
    for i in range(count // chunk):
        rows = pl.ds(i * chunk, chunk)
        behind = jnp.broadcast_to(query_tail[pl.ds(i * 8, 8)], shape) * keep
        added = jnp.zeros(shape, F32)
        for at in range(2):
            spill = jnp.sum(jnp.where(lane == row_of * SLOT + 10 + at, behind, 0.0), axis=2, keepdims=True)
            added = added + jnp.where(lane == at, spill, 0.0)
        query_part[rows, :] = query_part[rows, :] + added.reshape(chunk, LANES)

    wait_bytes(conv_dst, landed.at[CONV])
    wait_bytes(peak_dst, landed.at[PEAK])
    mine = lane == row_of
    for i in range(8):
        rows = pl.ds(i * chunk, chunk)
        peak = jnp.broadcast_to(peak_dst[pl.ds(i * 8, 8)], shape)
        peak = jnp.sum(jnp.where(mine, peak, 0.0), axis=2, keepdims=True)
        part = decoded(conv_dst[pl.ds(i * 8, 8)].astype(F32)) * peak
        out_ref[rows, :] = query_part[rows, :] * part.reshape(chunk, LANES)

    away = pl.ds(0, CTX - 1)
    for slot, source in ((GATE, gate_src), (EDGE, edge_src), (CONV, conv_src), (PEAK, peak_src)):
        wait_bytes(source.at[away], sent.at[slot])

    own_group = group == lax.rem(me, SHARE)

    @pl.when(own_group)
    def _():
        wait_bytes(filt_src.at[pl.ds(0, CTX // SHARE - 1)], sent.at[FILT])

    @pl.when(jnp.logical_not(own_group))
    def _():
        wait_bytes(filt_src.at[pl.ds(0, CTX // SHARE)], sent.at[FILT])

    for _ in range(1, SHARE):
        wait_bytes(share, sent.at[SIDE])
    tail.wait_send()


def halves(table):
    high = table.astype(jnp.bfloat16)
    return high, (table - high.astype(np.float64)).astype(jnp.bfloat16)


def tables():
    points = 2 * CTX * LANES
    j, s, k1, k2 = np.arange(CTX), np.arange(LANES), np.arange(CTX) + 0.5, np.arange(LANES)
    outer = 2 * math.pi / LANES * np.outer(k1, j)
    high, low = halves(np.concatenate([np.cos(outer), -np.sin(outer)], axis=0))
    fwd_across = np.concatenate([high, high, low, low], axis=1)
    high, low = halves(np.concatenate([np.cos(outer.T), -np.sin(outer.T)], axis=1) * (2.0 / points))
    inv_across = np.concatenate([high, high, low], axis=1)
    inner = 2 * math.pi / LANES * (np.outer(s, k2) % LANES)
    cos, sin = np.cos(inner), np.sin(inner)
    high, low = halves(np.block([[cos, -sin], [sin, cos]]))
    fwd_inner = np.concatenate([high, high, low], axis=0)
    high, low = halves(np.block([[cos, sin], [-sin, cos]]))
    inv_inner = np.concatenate([high, high, low], axis=0)
    angle = 2 * math.pi / points * np.outer(k1, s)
    turn = np.concatenate([np.cos(angle), -np.sin(angle)], axis=0).astype(np.float32)
    return fwd_across, fwd_inner, inv_inner, inv_across, turn


def solution(mesh):
    constants = tables()

    def body(features_in, short_weight, long_filter, skip_gain):
        operands = (features_in, short_weight.T, long_filter, skip_gain, *map(jnp.asarray, constants))
        count = long_filter.shape[0]
        rows = (CTX, OWN, LANES)
        row = (CTX, 1, LANES)
        own_copies = [
            (pltpu.SMEM if value.ndim == 1 else pltpu.VMEM)(value.shape, value.dtype) for value in operands
        ]
        scratch = own_copies + [
            pltpu.VMEM((3 * count, 8), F32),
            pltpu.VMEM((count, LANES), F32),
            pltpu.VMEM((CTX, LANES), F32),
            pltpu.VMEM((count, LANES), F32),
            pltpu.VMEM((count, LANES), F32),
            pltpu.VMEM((count, LANES), F32),
            pltpu.VMEM(rows, BF16), pltpu.VMEM(row, F32), pltpu.VMEM(rows, BF16),
            pltpu.VMEM(rows, BF16), pltpu.VMEM(row, F32), pltpu.VMEM((SHARE, CTX // SHARE, OWN, LANES), BF16),
            pltpu.VMEM(rows, BF16), pltpu.VMEM(row, F32),
            pltpu.VMEM(rows, BF16), pltpu.VMEM(row, F32),
            pltpu.VMEM(row, F32),
            pltpu.SemaphoreType.DMA((len(operands),)),
            pltpu.SemaphoreType.DMA((SLOTS,)),
            pltpu.SemaphoreType.DMA((SLOTS,)),
            pltpu.SemaphoreType.DMA((CTX // SHARE,)),
        ]
        operands = [pltpu.with_memory_space_constraint(value, pltpu.HBM) for value in operands]
        return pl.pallas_call(
            kernel,
            out_shape=jax.ShapeDtypeStruct((count, LANES), F32),
            in_specs=[pl.BlockSpec(memory_space=pltpu.HBM)] * len(operands),
            out_specs=pl.BlockSpec(memory_space=pltpu.VMEM),
            scratch_shapes=scratch,
            compiler_params=pltpu.CompilerParams(
                collective_id=0, has_side_effects=True, vmem_limit_bytes=48 * 1024 * 1024
            ),
        )(*operands)

    return jax.shard_map(
        body,
        mesh=mesh,
        in_specs=(P(None, ("dp", "ctx")), P(), P(None, "ctx"), P()),
        out_specs=P(None, ("dp", "ctx")),
        check_vma=False,
    )
```

```python
import functools
import math

import jax
import jax.numpy as jnp
import numpy as np
from jax import lax
from jax.experimental import pallas as pl
from jax.experimental.pallas import tpu as pltpu
from jax.sharding import PartitionSpec as P

MESH = pl.DeviceIdType.MESH
F32, BF16 = jnp.float32, jnp.bfloat16
RINGS = (16, 4)
CTX = RINGS[0] * RINGS[1]
SHARE = 4
LANES = 128
OWN = 8
LIFT = 2.0**7.5
SLOT = 16


def coded(value, largest):
    ratio = jnp.where(largest > 1e-30, LIFT / jnp.maximum(largest, 1e-30), 0.0)
    power = value * ratio
    for _ in range(4):
        power = power * power
    return jnp.where(value < 0, -power, power)


def decoded(code):
    size = jnp.abs(code)
    root = jnp.exp(jnp.log(jnp.maximum(size, 1e-37)) * (1.0 / 16.0)) * (1.0 / LIFT)
    root = jnp.where(size > 1e-37, root, 0.0)
    return jnp.where(code < 0, -root, root)


def farthest_first(index, extent):
    step = (index + 1) // 2
    return jnp.where(lax.rem(index, 2) == 0, extent // 2 + step, extent // 2 - step)


def each_peer(visit, begin=0):
    me = lax.axis_index("ctx")
    at_z, at_x = lax.div(me, RINGS[1]), lax.rem(me, RINGS[1])
    to_x = [lax.rem(at_x + step, RINGS[1]) for step in (2, 1, 3)]

    def plane(index, carry):
        step = lax.rem(index + begin, RINGS[0])
        step = lax.rem(at_z + farthest_first(step, RINGS[0]), RINGS[0])
        row = step * RINGS[1]
        for x in to_x:
            visit(row + x)

        @pl.when(step != at_z)
        def _():
            visit(row + at_x)

        return carry

    lax.fori_loop(0, RINGS[0], plane, 0)


def remote(source, target, sent, landed, **where):
    return pltpu.make_async_remote_copy(
        src_ref=source, dst_ref=target, send_sem=sent, recv_sem=landed, device_id=where, device_id_type=MESH
    )


def wait_bytes(ref, semaphore):
    pltpu.make_async_copy(ref, ref, semaphore).wait()


def split(value):
    high = value.astype(BF16)
    return high, (value - high.astype(F32)).astype(BF16)


def spectrum(blocks, across, inner, turn_re, turn_im):
    high, low = split(jnp.concatenate(blocks, axis=1))
    outer = jnp.dot(across, jnp.concatenate([high, low, high, low], axis=0), preferred_element_type=F32)
    rows = []
    for c in range(OWN):
        part = outer[:, c * LANES : (c + 1) * LANES]
        re, im = part[:CTX], part[CTX:]
        rows.append(jnp.concatenate([re * turn_re - im * turn_im, re * turn_im + im * turn_re], axis=1))
    high, low = split(jnp.concatenate(rows, axis=0))
    return jnp.dot(jnp.concatenate([high, low, high], axis=1), inner, preferred_element_type=F32)


def inverse(product, across, inner, turn_re, turn_im):
    high, low = split(product)
    mixed = jnp.dot(jnp.concatenate([high, low, high], axis=1), inner, preferred_element_type=F32)
    columns = []
    for c in range(OWN):
        part = mixed[c * CTX : (c + 1) * CTX]
        re, im = part[:, :LANES], part[:, LANES:]
        columns.append(jnp.concatenate([re * turn_re + im * turn_im, im * turn_re - re * turn_im], axis=0))
    high, low = split(jnp.concatenate(columns, axis=1))
    return jnp.dot(across, jnp.concatenate([high, low, high], axis=0), preferred_element_type=F32)


def lane_of(shape):
    return lax.broadcasted_iota(jnp.int32, shape, len(shape) - 1)


GATE, EDGE, FILT, CONV, PEAK, TAIL, SIDE, SLOTS = 0, 1, 2, 3, 4, 5, 6, 6 + SHARE


def kernel(
    feat_hbm, short_hbm, filt_hbm, skip_hbm, fwd_across_hbm, fwd_inner_hbm, inv_inner_hbm, inv_across_hbm, turn_hbm,
    out_ref,
    feat, short_flat, filt, skip, fwd_across, fwd_inner, inv_inner, inv_across, turn,
    short, edge_rows, edge_wide, plane, plane_h, query_part,
    gate_src, edge_src, filt_src, gate_dst, edge_dst, filt_dst,
    conv_src, peak_src, conv_dst, peak_dst, query_tail,
    load_sem, sent, landed, direct,
):
    me, part_at = lax.axis_index("ctx"), lax.axis_index("dp")
    member = lax.rem(part_at, SHARE)
    group = lax.rem(member - lax.rem(me, SHARE) + SHARE, SHARE)
    others = [part_at - member + lax.rem(member + step, SHARE) for step in range(1, SHARE)]
    barrier = pltpu.get_barrier_semaphore()
    each_peer(lambda peer: pl.semaphore_signal(barrier, inc=1, device_id={"ctx": peer}, device_id_type=MESH))
    for peer in others:
        pl.semaphore_signal(barrier, inc=1, device_id={"dp": peer}, device_id_type=MESH)

    pairs = (
        (feat_hbm, feat), (short_hbm, short_flat), (filt_hbm, filt), (skip_hbm, skip), (fwd_across_hbm, fwd_across),
        (fwd_inner_hbm, fwd_inner), (inv_inner_hbm, inv_inner), (inv_across_hbm, inv_across), (turn_hbm, turn),
    )
    loads = [pltpu.make_async_copy(source, target, load_sem.at[i]) for i, (source, target) in enumerate(pairs)]
    for load in loads:
        load.start()
    for load in loads:
        load.wait()

    count = OWN * CTX
    chunk = 8 * OWN
    lane = lane_of((chunk, LANES))
    for i in range(3 * count // LANES):
        taps = jnp.concatenate([short_flat[:, i * LANES : (i + 1) * LANES], jnp.zeros((5, LANES), F32)], axis=0)
        short[pl.ds(i * LANES, LANES), :] = taps.T

    def local_feature(row):
        rows = pl.ds(row, chunk)
        value = feat[rows, :].astype(F32)
        taps = short[rows, :]
        once, twice = pltpu.roll(value, 1, axis=1), pltpu.roll(value, 2, axis=1)
        near = taps[:, 1:2] * once
        far = taps[:, 2:3] * twice
        zero = jnp.zeros_like(value)
        inside = taps[:, 0:1] * value + jnp.where(lane >= 1, near, zero) + jnp.where(lane >= 2, far, zero)
        beyond = jnp.where(lane < 1, near, zero) + jnp.where(lane < 2, far, zero)
        return inside, beyond

    for i in range(count // chunk):
        row = i * chunk
        zero = jnp.zeros((chunk, LANES), F32)
        query, query_beyond = local_feature(row)
        query_part[pl.ds(row, chunk), :] = query
        key, key_beyond = local_feature(count + row)
        value, value_beyond = local_feature(2 * count + row)
        gated = key * value
        gated = jnp.where(lane >= 2, gated, zero)
        taps = filt[pl.ds(row, chunk), :]
        gated_peak = jnp.max(jnp.abs(gated), axis=1, keepdims=True)
        taps_peak = jnp.max(jnp.abs(taps), axis=1, keepdims=True)
        edge = (
            jnp.where(lane < 2, key, zero)
            + pltpu.roll(jnp.where(lane < 2, value, zero), 2, axis=1)
            + pltpu.roll(key_beyond, 4, axis=1)
            + pltpu.roll(value_beyond, 6, axis=1)
            + pltpu.roll(query_beyond, 10, axis=1)
        )
        edge = jnp.where(lane == 8, gated_peak, jnp.where(lane == 9, taps_peak, edge))
        edge_rows[pl.ds(row, chunk), :] = edge
        owners = pl.ds(i * 8, 8)
        gate_src[owners] = coded(gated, gated_peak).reshape(8, OWN, LANES).astype(BF16)
        filt_src[owners] = coded(taps, taps_peak).reshape(8, OWN, LANES).astype(BF16)

    wide = edge_rows[pl.ds(0, CTX, stride=OWN), :]
    for c in range(1, OWN):
        wide = wide + pltpu.roll(edge_rows[pl.ds(c, CTX, stride=OWN), :], SLOT * c, axis=1)
    edge_wide[...] = wide
    for q in range(CTX):
        edge_src[q] = edge_wide[q : q + 1, :]

    pl.semaphore_wait(barrier, CTX - 1 + SHARE - 1)

    filt_home = filt_dst.at[me % SHARE, me // SHARE]

    def send_filter(index, carry):
        place = lax.rem(me // SHARE + farthest_first(index, CTX // SHARE), CTX // SHARE)
        peer = place * SHARE + group

        @pl.when(peer != me)
        def _():
            remote(filt_src.at[peer], filt_home, sent.at[FILT], direct.at[me // SHARE], ctx=peer).start()

        @pl.when(peer == me)
        def _():
            pltpu.make_async_copy(filt_src.at[me], filt_home, direct.at[me // SHARE]).start()

        return carry

    lax.fori_loop(0, CTX // SHARE, send_filter, 0)

    def send_gated(peer):
        remote(gate_src.at[peer], gate_dst.at[me], sent.at[GATE], landed.at[GATE], ctx=peer).start()
        remote(edge_src.at[peer], edge_dst.at[me], sent.at[EDGE], landed.at[EDGE], ctx=peer).start()

    each_peer(send_gated, jnp.where(me < 2 * RINGS[1], 0, 7))
    pltpu.make_async_copy(gate_src.at[me], gate_dst.at[me], landed.at[GATE]).start()
    pltpu.make_async_copy(edge_src.at[me], edge_dst.at[me], landed.at[EDGE]).start()
    tail = remote(edge_src, query_tail, sent.at[TAIL], landed.at[TAIL], ctx=(me + 1) % CTX)
    tail.start()

    my_slot = me // SHARE

    def pass_on(index, carry):
        slot = lax.rem(my_slot + farthest_first(CTX // SHARE - 1 - index, CTX // SHARE), CTX // SHARE)
        block = filt_dst.at[group, slot]
        wait_bytes(block, direct.at[slot])
        for step, peer in enumerate(others):
            remote(block, block, sent.at[SIDE], landed.at[SIDE + 1 + step], dp=peer).start()
        return carry

    lax.fori_loop(0, CTX // SHARE, pass_on, 0)
    share = filt_dst.at[group]

    turn_re, turn_im = turn[:CTX], turn[CTX:]
    lane = lane_of((CTX, LANES))
    row_of = lax.broadcasted_iota(jnp.int32, (CTX, LANES), 0)
    wait_bytes(gate_dst, landed.at[GATE])
    for i in range(8):
        part = decoded(gate_dst[pl.ds(i * 8, 8)].astype(F32))
        plane[pl.ds(i * chunk, chunk), :] = part.reshape(chunk, LANES)
    wait_bytes(edge_dst, landed.at[EDGE])
    for p in range(CTX):
        edge_wide[p : p + 1, :] = edge_dst[p]
    edge = edge_wide[...]
    before = jnp.where(row_of >= 1, pltpu.roll(edge, 1, axis=0), 0.0)
    whole = edge + pltpu.roll(before, LANES - 4, axis=1)
    first = whole * pltpu.roll(whole, LANES - 2, axis=1)
    blocks = []
    for c in range(OWN):
        at = SLOT * c
        block = plane[pl.ds(c, CTX, stride=OWN), :] * edge[:, at + 8 : at + 9]
        block = jnp.where(lane == 0, first[:, at : at + 1], block)
        blocks.append(jnp.where(lane == 1, first[:, at + 1 : at + 2], block))
    seen = spectrum(blocks, fwd_across[...], fwd_inner[...], turn_re, turn_im)

    def unpack_filter(part):
        value = decoded(filt_dst[part].astype(F32))
        for k in range(CTX // SHARE):
            plane_h[pl.ds(pl.multiple_of((k * SHARE + part) * OWN, OWN), OWN), :] = value[k]

    unpack_filter(group)
    for step in range(1, SHARE):
        part = lax.rem(group - step + SHARE, SHARE)
        wait_bytes(filt_dst.at[part], landed.at[SIDE + step])
        unpack_filter(part)
    taps = [plane_h[pl.ds(c, CTX, stride=OWN), :] * edge[:, SLOT * c + 9 : SLOT * c + 10] for c in range(OWN)]
    response = spectrum(taps, fwd_across[...], fwd_inner[...], turn_re, turn_im)
    s_re, s_im = seen[:, :LANES], seen[:, LANES:]
    r_re, r_im = response[:, :LANES], response[:, LANES:]
    product = jnp.concatenate([s_re * r_re - s_im * r_im, s_re * r_im + s_im * r_re], axis=1)
    result = inverse(product, inv_across[...], inv_inner[...], turn_re, turn_im)

    peaks = jnp.zeros((CTX, LANES), F32)
    for c in range(OWN):
        part = result[:, c * LANES : (c + 1) * LANES] + skip[me * OWN + c] * blocks[c]
        peak = jnp.max(jnp.abs(part), axis=1, keepdims=True)
        peaks = jnp.where(lane == c, peak, peaks)
        plane[pl.ds(c, CTX, stride=OWN), :] = coded(part, peak)
    edge_wide[...] = peaks
    for q in range(CTX):
        peak_src[q] = edge_wide[q : q + 1, :]
    for i in range(8):
        conv_src[pl.ds(i * 8, 8)] = plane[pl.ds(i * chunk, chunk), :].reshape(8, OWN, LANES).astype(BF16)

    def send_result(peer):
        remote(conv_src.at[peer], conv_dst.at[me], sent.at[CONV], landed.at[CONV], ctx=peer).start()
        remote(peak_src.at[peer], peak_dst.at[me], sent.at[PEAK], landed.at[PEAK], ctx=peer).start()

    each_peer(send_result)
    pltpu.make_async_copy(conv_src.at[me], conv_dst.at[me], landed.at[CONV]).start()
    pltpu.make_async_copy(peak_src.at[me], peak_dst.at[me], landed.at[PEAK]).start()

    tail.wait_recv()
    shape = (8, OWN, LANES)
    lane = lane_of(shape)
    row_of = lax.broadcasted_iota(jnp.int32, shape, 1)
    keep = jnp.where(me > 0, 1.0, 0.0)
    for i in range(count // chunk):
        rows = pl.ds(i * chunk, chunk)
        behind = jnp.broadcast_to(query_tail[pl.ds(i * 8, 8)], shape) * keep
        added = jnp.zeros(shape, F32)
        for at in range(2):
            spill = jnp.sum(jnp.where(lane == row_of * SLOT + 10 + at, behind, 0.0), axis=2, keepdims=True)
            added = added + jnp.where(lane == at, spill, 0.0)
        query_part[rows, :] = query_part[rows, :] + added.reshape(chunk, LANES)

    wait_bytes(conv_dst, landed.at[CONV])
    wait_bytes(peak_dst, landed.at[PEAK])
    mine = lane == row_of
    for i in range(8):
        rows = pl.ds(i * chunk, chunk)
        peak = jnp.broadcast_to(peak_dst[pl.ds(i * 8, 8)], shape)
        peak = jnp.sum(jnp.where(mine, peak, 0.0), axis=2, keepdims=True)
        part = decoded(conv_dst[pl.ds(i * 8, 8)].astype(F32)) * peak
        out_ref[rows, :] = query_part[rows, :] * part.reshape(chunk, LANES)

    away = pl.ds(0, CTX - 1)
    for slot, source in ((GATE, gate_src), (EDGE, edge_src), (CONV, conv_src), (PEAK, peak_src)):
        wait_bytes(source.at[away], sent.at[slot])

    own_group = group == lax.rem(me, SHARE)

    @pl.when(own_group)
    def _():
        wait_bytes(filt_src.at[pl.ds(0, CTX // SHARE - 1)], sent.at[FILT])

    @pl.when(jnp.logical_not(own_group))
    def _():
        wait_bytes(filt_src.at[pl.ds(0, CTX // SHARE)], sent.at[FILT])

    for _ in range(1, SHARE):
        wait_bytes(share, sent.at[SIDE])
    tail.wait_send()


def halves(table):
    high = table.astype(jnp.bfloat16)
    return high, (table - high.astype(np.float64)).astype(jnp.bfloat16)


def tables():
    points = 2 * CTX * LANES
    j, s, k1, k2 = np.arange(CTX), np.arange(LANES), np.arange(CTX) + 0.5, np.arange(LANES)
    outer = 2 * math.pi / LANES * np.outer(k1, j)
    high, low = halves(np.concatenate([np.cos(outer), -np.sin(outer)], axis=0))
    fwd_across = np.concatenate([high, high, low, low], axis=1)
    high, low = halves(np.concatenate([np.cos(outer.T), -np.sin(outer.T)], axis=1) * (2.0 / points))
    inv_across = np.concatenate([high, high, low], axis=1)
    inner = 2 * math.pi / LANES * (np.outer(s, k2) % LANES)
    cos, sin = np.cos(inner), np.sin(inner)
    high, low = halves(np.block([[cos, -sin], [sin, cos]]))
    fwd_inner = np.concatenate([high, high, low], axis=0)
    high, low = halves(np.block([[cos, sin], [-sin, cos]]))
    inv_inner = np.concatenate([high, high, low], axis=0)
    angle = 2 * math.pi / points * np.outer(k1, s)
    turn = np.concatenate([np.cos(angle), -np.sin(angle)], axis=0).astype(np.float32)
    return fwd_across, fwd_inner, inv_inner, inv_across, turn


def solution(mesh):
    constants = tables()

    def body(features_in, short_weight, long_filter, skip_gain):
        operands = (features_in, short_weight.T, long_filter, skip_gain, *map(jnp.asarray, constants))
        count = long_filter.shape[0]
        rows = (CTX, OWN, LANES)
        row = (CTX, 1, LANES)
        own_copies = [
            (pltpu.SMEM if value.ndim == 1 else pltpu.VMEM)(value.shape, value.dtype) for value in operands
        ]
        scratch = own_copies + [
            pltpu.VMEM((3 * count, 8), F32),
            pltpu.VMEM((count, LANES), F32),
            pltpu.VMEM((CTX, LANES), F32),
            pltpu.VMEM((count, LANES), F32),
            pltpu.VMEM((count, LANES), F32),
            pltpu.VMEM((count, LANES), F32),
            pltpu.VMEM(rows, BF16), pltpu.VMEM(row, F32), pltpu.VMEM(rows, BF16),
            pltpu.VMEM(rows, BF16), pltpu.VMEM(row, F32), pltpu.VMEM((SHARE, CTX // SHARE, OWN, LANES), BF16),
            pltpu.VMEM(rows, BF16), pltpu.VMEM(row, F32),
            pltpu.VMEM(rows, BF16), pltpu.VMEM(row, F32),
            pltpu.VMEM(row, F32),
            pltpu.SemaphoreType.DMA((len(operands),)),
            pltpu.SemaphoreType.DMA((SLOTS,)),
            pltpu.SemaphoreType.DMA((SLOTS,)),
            pltpu.SemaphoreType.DMA((CTX // SHARE,)),
        ]
        operands = [pltpu.with_memory_space_constraint(value, pltpu.HBM) for value in operands]
        return pl.pallas_call(
            kernel,
            out_shape=jax.ShapeDtypeStruct((count, LANES), F32),
            in_specs=[pl.BlockSpec(memory_space=pltpu.HBM)] * len(operands),
            out_specs=pl.BlockSpec(memory_space=pltpu.VMEM),
            scratch_shapes=scratch,
            compiler_params=pltpu.CompilerParams(
                collective_id=0, has_side_effects=True, vmem_limit_bytes=48 * 1024 * 1024
            ),
        )(*operands)

    return jax.shard_map(
        body,
        mesh=mesh,
        in_specs=(P(None, ("dp", "ctx")), P(), P(None, "ctx"), P()),
        out_specs=P(None, ("dp", "ctx")),
        check_vma=False,
    )
```

```python
import functools
import math

import jax
import jax.numpy as jnp
import numpy as np
from jax import lax
from jax.experimental import pallas as pl
from jax.experimental.pallas import tpu as pltpu
from jax.sharding import PartitionSpec as P

MESH = pl.DeviceIdType.MESH
F32, BF16 = jnp.float32, jnp.bfloat16
RINGS = (16, 4)
CTX = RINGS[0] * RINGS[1]
SHARE = 4
LANES = 128
OWN = 8
LIFT = 2.0**7.5
SLOT = 16


def coded(value, largest):
    ratio = jnp.where(largest > 1e-30, LIFT / jnp.maximum(largest, 1e-30), 0.0)
    power = value * ratio
    for _ in range(4):
        power = power * power
    return jnp.where(value < 0, -power, power)


def decoded(code):
    size = jnp.abs(code)
    root = jnp.exp(jnp.log(jnp.maximum(size, 1e-37)) * (1.0 / 16.0)) * (1.0 / LIFT)
    root = jnp.where(size > 1e-37, root, 0.0)
    return jnp.where(code < 0, -root, root)


def farthest_first(index, extent):
    step = (index + 1) // 2
    return jnp.where(lax.rem(index, 2) == 0, extent // 2 + step, extent // 2 - step)


def each_peer(visit, begin=0):
    me = lax.axis_index("ctx")
    at_z, at_x = lax.div(me, RINGS[1]), lax.rem(me, RINGS[1])
    to_x = [lax.rem(at_x + step, RINGS[1]) for step in (2, 1, 3)]

    def plane(index, carry):
        step = lax.rem(index + begin, RINGS[0])
        step = lax.rem(at_z + farthest_first(step, RINGS[0]), RINGS[0])
        row = step * RINGS[1]
        for x in to_x:
            visit(row + x)

        @pl.when(step != at_z)
        def _():
            visit(row + at_x)

        return carry

    lax.fori_loop(0, RINGS[0], plane, 0)


def remote(source, target, sent, landed, **where):
    return pltpu.make_async_remote_copy(
        src_ref=source, dst_ref=target, send_sem=sent, recv_sem=landed, device_id=where, device_id_type=MESH
    )


def wait_bytes(ref, semaphore):
    pltpu.make_async_copy(ref, ref, semaphore).wait()


def split(value):
    high = value.astype(BF16)
    return high, (value - high.astype(F32)).astype(BF16)


def spectrum(blocks, across, inner, turn_re, turn_im):
    high, low = split(jnp.concatenate(blocks, axis=1))
    outer = jnp.dot(across, jnp.concatenate([high, low, high, low], axis=0), preferred_element_type=F32)
    rows = []
    for c in range(OWN):
        part = outer[:, c * LANES : (c + 1) * LANES]
        re, im = part[:CTX], part[CTX:]
        rows.append(jnp.concatenate([re * turn_re - im * turn_im, re * turn_im + im * turn_re], axis=1))
    high, low = split(jnp.concatenate(rows, axis=0))
    return jnp.dot(jnp.concatenate([high, low, high], axis=1), inner, preferred_element_type=F32)


def inverse(product, across, inner, turn_re, turn_im):
    high, low = split(product)
    mixed = jnp.dot(jnp.concatenate([high, low, high], axis=1), inner, preferred_element_type=F32)
    columns = []
    for c in range(OWN):
        part = mixed[c * CTX : (c + 1) * CTX]
        re, im = part[:, :LANES], part[:, LANES:]
        columns.append(jnp.concatenate([re * turn_re + im * turn_im, im * turn_re - re * turn_im], axis=0))
    high, low = split(jnp.concatenate(columns, axis=1))
    sums = jnp.dot(across, jnp.concatenate([high, low], axis=0), preferred_element_type=F32)
    return sums[:CTX] + sums[CTX:]


def lane_of(shape):
    return lax.broadcasted_iota(jnp.int32, shape, len(shape) - 1)


GATE, EDGE, FILT, CONV, PEAK, TAIL, SIDE, SLOTS = 0, 1, 2, 3, 4, 5, 6, 6 + SHARE


def kernel(
    feat_hbm, short_hbm, filt_hbm, skip_hbm, fwd_across_hbm, fwd_inner_hbm, inv_inner_hbm, inv_across_hbm, turn_hbm,
    out_ref,
    feat, short_flat, filt, skip, fwd_across, fwd_inner, inv_inner, inv_across, turn,
    short, edge_rows, edge_wide, plane, plane_h, query_part,
    gate_src, edge_src, filt_src, gate_dst, edge_dst, filt_dst,
    conv_src, peak_src, conv_dst, peak_dst, query_tail,
    load_sem, sent, landed, direct,
):
    me, part_at = lax.axis_index("ctx"), lax.axis_index("dp")
    member = lax.rem(part_at, SHARE)
    group = lax.rem(member - lax.rem(me, SHARE) + SHARE, SHARE)
    others = [part_at - member + lax.rem(member + step, SHARE) for step in range(1, SHARE)]
    barrier = pltpu.get_barrier_semaphore()
    each_peer(lambda peer: pl.semaphore_signal(barrier, inc=1, device_id={"ctx": peer}, device_id_type=MESH))
    for peer in others:
        pl.semaphore_signal(barrier, inc=1, device_id={"dp": peer}, device_id_type=MESH)

    pairs = (
        (feat_hbm, feat), (short_hbm, short_flat), (filt_hbm, filt), (skip_hbm, skip), (fwd_across_hbm, fwd_across),
        (fwd_inner_hbm, fwd_inner), (inv_inner_hbm, inv_inner), (inv_across_hbm, inv_across), (turn_hbm, turn),
    )
    loads = [pltpu.make_async_copy(source, target, load_sem.at[i]) for i, (source, target) in enumerate(pairs)]
    for load in loads:
        load.start()
    for load in loads:
        load.wait()

    count = OWN * CTX
    chunk = 8 * OWN
    lane = lane_of((chunk, LANES))
    for i in range(3 * count // LANES):
        taps = jnp.concatenate([short_flat[:, i * LANES : (i + 1) * LANES], jnp.zeros((5, LANES), F32)], axis=0)
        short[pl.ds(i * LANES, LANES), :] = taps.T

    def local_feature(row):
        rows = pl.ds(row, chunk)
        value = feat[rows, :].astype(F32)
        taps = short[rows, :]
        once, twice = pltpu.roll(value, 1, axis=1), pltpu.roll(value, 2, axis=1)
        near = taps[:, 1:2] * once
        far = taps[:, 2:3] * twice
        zero = jnp.zeros_like(value)
        inside = taps[:, 0:1] * value + jnp.where(lane >= 1, near, zero) + jnp.where(lane >= 2, far, zero)
        beyond = jnp.where(lane < 1, near, zero) + jnp.where(lane < 2, far, zero)
        return inside, beyond

    for i in range(count // chunk):
        row = i * chunk
        zero = jnp.zeros((chunk, LANES), F32)
        query, query_beyond = local_feature(row)
        query_part[pl.ds(row, chunk), :] = query
        key, key_beyond = local_feature(count + row)
        value, value_beyond = local_feature(2 * count + row)
        gated = key * value
        gated = jnp.where(lane >= 2, gated, zero)
        taps = filt[pl.ds(row, chunk), :]
        gated_peak = jnp.max(jnp.abs(gated), axis=1, keepdims=True)
        taps_peak = jnp.max(jnp.abs(taps), axis=1, keepdims=True)
        edge = (
            jnp.where(lane < 2, key, zero)
            + pltpu.roll(jnp.where(lane < 2, value, zero), 2, axis=1)
            + pltpu.roll(key_beyond, 4, axis=1)
            + pltpu.roll(value_beyond, 6, axis=1)
            + pltpu.roll(query_beyond, 10, axis=1)
        )
        edge = jnp.where(lane == 8, gated_peak, jnp.where(lane == 9, taps_peak, edge))
        edge_rows[pl.ds(row, chunk), :] = edge
        owners = pl.ds(i * 8, 8)
        gate_src[owners] = coded(gated, gated_peak).reshape(8, OWN, LANES).astype(BF16)
        filt_src[owners] = coded(taps, taps_peak).reshape(8, OWN, LANES).astype(BF16)

    wide = edge_rows[pl.ds(0, CTX, stride=OWN), :]
    for c in range(1, OWN):
        wide = wide + pltpu.roll(edge_rows[pl.ds(c, CTX, stride=OWN), :], SLOT * c, axis=1)
    edge_wide[...] = wide
    for q in range(CTX):
        edge_src[q] = edge_wide[q : q + 1, :]

    pl.semaphore_wait(barrier, CTX - 1 + SHARE - 1)

    filt_home = filt_dst.at[me % SHARE, me // SHARE]

    def send_filter(index, carry):
        place = lax.rem(me // SHARE + farthest_first(index, CTX // SHARE), CTX // SHARE)
        peer = place * SHARE + group

        @pl.when(peer != me)
        def _():
            remote(filt_src.at[peer], filt_home, sent.at[FILT], direct.at[me // SHARE], ctx=peer).start()

        @pl.when(peer == me)
        def _():
            pltpu.make_async_copy(filt_src.at[me], filt_home, direct.at[me // SHARE]).start()

        return carry

    lax.fori_loop(0, CTX // SHARE, send_filter, 0)

    def send_gated(peer):
        remote(gate_src.at[peer], gate_dst.at[me], sent.at[GATE], landed.at[GATE], ctx=peer).start()
        remote(edge_src.at[peer], edge_dst.at[me], sent.at[EDGE], landed.at[EDGE], ctx=peer).start()

    each_peer(send_gated, jnp.where(me < 2 * RINGS[1], 0, 7))
    pltpu.make_async_copy(gate_src.at[me], gate_dst.at[me], landed.at[GATE]).start()
    pltpu.make_async_copy(edge_src.at[me], edge_dst.at[me], landed.at[EDGE]).start()
    tail = remote(edge_src, query_tail, sent.at[TAIL], landed.at[TAIL], ctx=(me + 1) % CTX)
    tail.start()

    my_slot = me // SHARE

    def pass_on(index, carry):
        slot = lax.rem(my_slot + farthest_first(CTX // SHARE - 1 - index, CTX // SHARE), CTX // SHARE)
        block = filt_dst.at[group, slot]
        wait_bytes(block, direct.at[slot])
        for step, peer in enumerate(others):
            remote(block, block, sent.at[SIDE], landed.at[SIDE + 1 + step], dp=peer).start()
        return carry

    lax.fori_loop(0, CTX // SHARE, pass_on, 0)
    share = filt_dst.at[group]

    turn_re, turn_im = turn[:CTX], turn[CTX:]
    lane = lane_of((CTX, LANES))
    row_of = lax.broadcasted_iota(jnp.int32, (CTX, LANES), 0)
    wait_bytes(gate_dst, landed.at[GATE])
    for i in range(8):
        part = decoded(gate_dst[pl.ds(i * 8, 8)].astype(F32))
        plane[pl.ds(i * chunk, chunk), :] = part.reshape(chunk, LANES)
    wait_bytes(edge_dst, landed.at[EDGE])
    for p in range(CTX):
        edge_wide[p : p + 1, :] = edge_dst[p]
    edge = edge_wide[...]
    before = jnp.where(row_of >= 1, pltpu.roll(edge, 1, axis=0), 0.0)
    whole = edge + pltpu.roll(before, LANES - 4, axis=1)
    first = whole * pltpu.roll(whole, LANES - 2, axis=1)
    blocks = []
    for c in range(OWN):
        at = SLOT * c
        block = plane[pl.ds(c, CTX, stride=OWN), :] * edge[:, at + 8 : at + 9]
        block = jnp.where(lane == 0, first[:, at : at + 1], block)
        blocks.append(jnp.where(lane == 1, first[:, at + 1 : at + 2], block))
    seen = spectrum(blocks, fwd_across[...], fwd_inner[...], turn_re, turn_im)

    def unpack_filter(part):
        value = decoded(filt_dst[part].astype(F32))
        for k in range(CTX // SHARE):
            plane_h[pl.ds(pl.multiple_of((k * SHARE + part) * OWN, OWN), OWN), :] = value[k]

    unpack_filter(group)
    for step in range(1, SHARE):
        part = lax.rem(group - step + SHARE, SHARE)
        wait_bytes(filt_dst.at[part], landed.at[SIDE + step])
        unpack_filter(part)
    taps = [plane_h[pl.ds(c, CTX, stride=OWN), :] * edge[:, SLOT * c + 9 : SLOT * c + 10] for c in range(OWN)]
    response = spectrum(taps, fwd_across[...], fwd_inner[...], turn_re, turn_im)
    s_re, s_im = seen[:, :LANES], seen[:, LANES:]
    r_re, r_im = response[:, :LANES], response[:, LANES:]
    product = jnp.concatenate([s_re * r_re - s_im * r_im, s_re * r_im + s_im * r_re], axis=1)
    result = inverse(product, inv_across[...], inv_inner[...], turn_re, turn_im)

    peaks = jnp.zeros((CTX, LANES), F32)
    for c in range(OWN):
        part = result[:, c * LANES : (c + 1) * LANES] + skip[me * OWN + c] * blocks[c]
        peak = jnp.max(jnp.abs(part), axis=1, keepdims=True)
        peaks = jnp.where(lane == c, peak, peaks)
        plane[pl.ds(c, CTX, stride=OWN), :] = coded(part, peak)
    edge_wide[...] = peaks
    for q in range(CTX):
        peak_src[q] = edge_wide[q : q + 1, :]
    for i in range(8):
        conv_src[pl.ds(i * 8, 8)] = plane[pl.ds(i * chunk, chunk), :].reshape(8, OWN, LANES).astype(BF16)

    def send_result(peer):
        remote(conv_src.at[peer], conv_dst.at[me], sent.at[CONV], landed.at[CONV], ctx=peer).start()
        remote(peak_src.at[peer], peak_dst.at[me], sent.at[PEAK], landed.at[PEAK], ctx=peer).start()

    each_peer(send_result)
    pltpu.make_async_copy(conv_src.at[me], conv_dst.at[me], landed.at[CONV]).start()
    pltpu.make_async_copy(peak_src.at[me], peak_dst.at[me], landed.at[PEAK]).start()

    tail.wait_recv()
    shape = (8, OWN, LANES)
    lane = lane_of(shape)
    row_of = lax.broadcasted_iota(jnp.int32, shape, 1)
    keep = jnp.where(me > 0, 1.0, 0.0)
    for i in range(count // chunk):
        rows = pl.ds(i * chunk, chunk)
        behind = jnp.broadcast_to(query_tail[pl.ds(i * 8, 8)], shape) * keep
        added = jnp.zeros(shape, F32)
        for at in range(2):
            spill = jnp.sum(jnp.where(lane == row_of * SLOT + 10 + at, behind, 0.0), axis=2, keepdims=True)
            added = added + jnp.where(lane == at, spill, 0.0)
        query_part[rows, :] = query_part[rows, :] + added.reshape(chunk, LANES)

    wait_bytes(conv_dst, landed.at[CONV])
    wait_bytes(peak_dst, landed.at[PEAK])
    mine = lane == row_of
    for i in range(8):
        rows = pl.ds(i * chunk, chunk)
        peak = jnp.broadcast_to(peak_dst[pl.ds(i * 8, 8)], shape)
        peak = jnp.sum(jnp.where(mine, peak, 0.0), axis=2, keepdims=True)
        part = decoded(conv_dst[pl.ds(i * 8, 8)].astype(F32)) * peak
        out_ref[rows, :] = query_part[rows, :] * part.reshape(chunk, LANES)

    away = pl.ds(0, CTX - 1)
    for slot, source in ((GATE, gate_src), (EDGE, edge_src), (CONV, conv_src), (PEAK, peak_src)):
        wait_bytes(source.at[away], sent.at[slot])

    own_group = group == lax.rem(me, SHARE)

    @pl.when(own_group)
    def _():
        wait_bytes(filt_src.at[pl.ds(0, CTX // SHARE - 1)], sent.at[FILT])

    @pl.when(jnp.logical_not(own_group))
    def _():
        wait_bytes(filt_src.at[pl.ds(0, CTX // SHARE)], sent.at[FILT])

    for _ in range(1, SHARE):
        wait_bytes(share, sent.at[SIDE])
    tail.wait_send()


def halves(table):
    high = table.astype(jnp.bfloat16)
    return high, (table - high.astype(np.float64)).astype(jnp.bfloat16)


def tables():
    points = 2 * CTX * LANES
    j, s, k1, k2 = np.arange(CTX), np.arange(LANES), np.arange(CTX) + 0.5, np.arange(LANES)
    outer = 2 * math.pi / LANES * np.outer(k1, j)
    high, low = halves(np.concatenate([np.cos(outer), -np.sin(outer)], axis=0))
    fwd_across = np.concatenate([high, high, low, low], axis=1)
    high, low = halves(np.concatenate([np.cos(outer.T), -np.sin(outer.T)], axis=1) * (2.0 / points))
    inv_across = np.block([[high, high], [low, np.zeros_like(low)]])
    inner = 2 * math.pi / LANES * (np.outer(s, k2) % LANES)
    cos, sin = np.cos(inner), np.sin(inner)
    high, low = halves(np.block([[cos, -sin], [sin, cos]]))
    fwd_inner = np.concatenate([high, high, low], axis=0)
    high, low = halves(np.block([[cos, sin], [-sin, cos]]))
    inv_inner = np.concatenate([high, high, low], axis=0)
    angle = 2 * math.pi / points * np.outer(k1, s)
    turn = np.concatenate([np.cos(angle), -np.sin(angle)], axis=0).astype(np.float32)
    return fwd_across, fwd_inner, inv_inner, inv_across, turn


def solution(mesh):
    constants = tables()

    def body(features_in, short_weight, long_filter, skip_gain):
        operands = (features_in, short_weight.T, long_filter, skip_gain, *map(jnp.asarray, constants))
        count = long_filter.shape[0]
        rows = (CTX, OWN, LANES)
        row = (CTX, 1, LANES)
        own_copies = [
            (pltpu.SMEM if value.ndim == 1 else pltpu.VMEM)(value.shape, value.dtype) for value in operands
        ]
        scratch = own_copies + [
            pltpu.VMEM((3 * count, 8), F32),
            pltpu.VMEM((count, LANES), F32),
            pltpu.VMEM((CTX, LANES), F32),
            pltpu.VMEM((count, LANES), F32),
            pltpu.VMEM((count, LANES), F32),
            pltpu.VMEM((count, LANES), F32),
            pltpu.VMEM(rows, BF16), pltpu.VMEM(row, F32), pltpu.VMEM(rows, BF16),
            pltpu.VMEM(rows, BF16), pltpu.VMEM(row, F32), pltpu.VMEM((SHARE, CTX // SHARE, OWN, LANES), BF16),
            pltpu.VMEM(rows, BF16), pltpu.VMEM(row, F32),
            pltpu.VMEM(rows, BF16), pltpu.VMEM(row, F32),
            pltpu.VMEM(row, F32),
            pltpu.SemaphoreType.DMA((len(operands),)),
            pltpu.SemaphoreType.DMA((SLOTS,)),
            pltpu.SemaphoreType.DMA((SLOTS,)),
            pltpu.SemaphoreType.DMA((CTX // SHARE,)),
        ]
        operands = [pltpu.with_memory_space_constraint(value, pltpu.HBM) for value in operands]
        return pl.pallas_call(
            kernel,
            out_shape=jax.ShapeDtypeStruct((count, LANES), F32),
            in_specs=[pl.BlockSpec(memory_space=pltpu.HBM)] * len(operands),
            out_specs=pl.BlockSpec(memory_space=pltpu.VMEM),
            scratch_shapes=scratch,
            compiler_params=pltpu.CompilerParams(
                collective_id=0, has_side_effects=True, vmem_limit_bytes=48 * 1024 * 1024
            ),
        )(*operands)

    return jax.shard_map(
        body,
        mesh=mesh,
        in_specs=(P(None, ("dp", "ctx")), P(), P(None, "ctx"), P()),
        out_specs=P(None, ("dp", "ctx")),
        check_vma=False,
    )
```
